512 devices in a mesh: row: 16 (over z), col: 32 (over y, x, core).
Axes of the slice: x: 4, y: 4, z: 16, core: 2. Of those that a mesh axis runs over, the one named last changes fastest.
Arguments:
- dosage_words: int32 [8192, 8192], P('row', 'col'), may hold values from 0 to 2730, as said below
- sample_weight: float32 [8192], P('row'), may hold values from 0.3 to 3
- variant_weight: float32 [49152], P('col'), may hold values from 0.7 to 12.6, as said below
- omega: bfloat16 [49152, 128], P('col'), may hold values from -6 to 6
Outputs:
- basis: float32 [8192, 128], P(('row', 'col'))
- right_basis: float32 [49152, 128], P('col')
- projection: float32 [49152, 128], P('col', 'row')
The draws below stay inside these ranges and needn't reach their ends.
Inputs may be any that keep to these rules, and one draw needn't show every extreme that they name: `dosage_words`: each word holds 6 dosages of 0, 1 or 2 in two bits each, laid out as the first step says. `variant_weight`: positive weights of the variants.
All inputs are finite; a program needn't handle non-finite values.
Results may differ from the reference program's by a relative error of at most 0.024.
Values may be sent and summed in bfloat16 or wider, within the bound.
No kernel may reach another device: no remote copies, remote signals or barrier semaphores. Data moves between devices by JAX's collectives and lax.ppermute only.
A program may use at most 64 MiB of HBM per device.

```python
import math
import jax
import jax.numpy as jnp
from jax import lax

COLS_DEV = 1536
RANK = 128
ROWS = 8192
COLS = 49152
N_COL = 32


def draw_dosage_words(key, part):
    key = jax.random.fold_in(key, 7)
    level_key, digit_key, place_key = jax.random.split(key, 3)
    width = COLS // 6
    levels = jax.random.randint(level_key, (6, width), 2, 17)
    words = jnp.zeros((ROWS, width), jnp.int32)
    for place in range(6):
        uniform_ints = jax.random.randint(jax.random.fold_in(digit_key, place), (ROWS, width), 0, levels[place][None, :])
        digit = (uniform_ints == 0).astype(jnp.int32) + (uniform_ints <= 1).astype(jnp.int32)
        words = words + digit * 4 ** place
    top_row = jax.random.randint(place_key, (width,), 0, ROWS)
    offset = jax.random.randint(jax.random.fold_in(place_key, 1), (width,), 1, ROWS)
    low_row = (top_row + offset) % ROWS
    row_ids = jnp.arange(ROWS, dtype=jnp.int32)[:, None]
    words = jnp.where(row_ids == top_row[None, :], 2730, words)
    words = jnp.where(row_ids == low_row[None, :], 0, words)
    return words


def draw_variant_weight(key, part):
    key = jax.random.fold_in(key, 11)
    rise = 2.0
    index = jnp.arange(COLS, dtype=jnp.int32)
    blocks = COLS // COLS_DEV
    outer = (index // COLS_DEV).astype(jnp.float32) / blocks
    inner = (index % COLS_DEV).astype(jnp.float32) / COLS_DEV
    trend = jnp.exp(math.log(rise) * (outer + inner))
    jitter = jnp.exp(jax.random.uniform(key, (COLS,), jnp.float32, math.log(0.7), math.log(1.4)))
    return (trend * jitter).astype(jnp.float32)


def block_scale(stream_key, extent, pieces, low, largest):
    factor_of = 1.0
    for axis_at, blocks in pieces:
        steps = jax.random.uniform(jax.random.fold_in(jax.random.fold_in(stream_key, 6), axis_at), (blocks,), jnp.float32, low / len(pieces), largest / len(pieces))
        factor_of = factor_of * jnp.repeat(jnp.exp(steps), extent[axis_at] // blocks).reshape((-1,) + (1,) * (len(extent) - 1 - axis_at))
    return factor_of


def scatter_about(rng, dims, deviation, reach, shards=(), kind=jnp.bfloat16):
    loudness = block_scale(rng, dims, shards, -0.22, 0.18) if shards else 1.0
    entries = jax.random.normal(rng, dims, jnp.float32) * deviation * loudness
    return jnp.minimum(jnp.maximum(entries, -reach), reach).astype(kind)


def setup_inputs(seed: int = 0) -> dict:
    key_list = jax.random.split(jax.random.key(seed), 5)
    return {
        "dosage_words": draw_dosage_words(jax.random.fold_in(key_list[4], 71), 0),
        "sample_weight": jnp.clip(jnp.exp(math.log(3.0) - 2.3025851 * jax.random.uniform(key_list[1], (ROWS,), jnp.float32) ** block_scale(key_list[1], (ROWS,), ((0, 16),), -0.2, 0.2)), 0.3, 3.0),
        "variant_weight": draw_variant_weight(jax.random.fold_in(key_list[4], 71), 0),
        "omega": scatter_about(key_list[3], (COLS, RANK), 1.0, 6.0, ((0, 32),)),
    }


EPSILON = 1e-05

def unpack(words):
    shifts = 2 * jnp.arange(6, dtype=jnp.int32)
    parts = jnp.bitwise_and(jnp.right_shift(words[None, :, :], shifts[:, None, None]), 3)
    return jnp.transpose(parts, (1, 0, 2)).reshape(words.shape[0], 6 * words.shape[1]).astype(jnp.float32)

def standard(dosage, column_mean, column_scale, weight, column_weight):
    return ((dosage - column_mean) * column_scale * weight[:, None] * column_weight).astype(jnp.bfloat16)

def orthonormal(panel, gram_sum):
    lower = jnp.linalg.cholesky(gram_sum)
    identity = jnp.eye(gram_sum.shape[0], dtype=jnp.float32)
    inverse = lax.linalg.triangular_solve(lower, identity, left_side=True, lower=True)
    return jnp.dot(panel, inverse.T, precision=lax.Precision.HIGHEST)

def orth_full(panel):
    gram_sum = jnp.dot(panel.T, panel, precision=lax.Precision.HIGHEST)
    return orthonormal(panel, gram_sum)

def reference(dosage_words, sample_weight, variant_weight, omega):
    blocks = N_COL
    width = COLS_DEV // 6
    words = dosage_words.reshape(ROWS, blocks, width).transpose(1, 0, 2)
    panels = omega.reshape(blocks, COLS_DEV, RANK)
    column_weights = variant_weight.reshape(blocks, COLS_DEV)
    indices = jnp.arange(blocks, dtype=jnp.int32)

    def moments(block):
        dosage = unpack(block)
        return (lax.optimization_barrier(jnp.sum(dosage, axis=0)), lax.optimization_barrier(jnp.sum(dosage * dosage, axis=0)))
    totals, squares = lax.map(moments, words)
    column_mean = totals / ROWS
    column_scale = lax.rsqrt(squares / ROWS - column_mean * column_mean + EPSILON)

    def matrix(index):
        return standard(unpack(words[index]), column_mean[index], column_scale[index], sample_weight, column_weights[index])

    def forward(panel_blocks):

        def advance(carry, index):
            product = jnp.dot(matrix(index).astype(jnp.float32), panel_blocks[index].astype(jnp.float32), preferred_element_type=jnp.float32)
            return (carry + product, None)
        result, unused = lax.scan(advance, jnp.zeros((ROWS, RANK), jnp.float32), indices)
        return result

    def backward(basis_half):

        def one_block(index):
            return lax.dot_general(matrix(index).astype(jnp.float32), basis_half.astype(jnp.float32), (((0,), (0,)), ((), ())), preferred_element_type=jnp.float32)
        return lax.map(one_block, indices).reshape(COLS, RANK)
    first = orth_full(forward(panels)).astype(jnp.bfloat16)
    back = backward(first)
    right_full = orth_full(back)
    right = right_full.astype(jnp.bfloat16).reshape(blocks, COLS_DEV, RANK)
    second = orth_full(forward(right))
    projection = backward(second.astype(jnp.bfloat16))
    return (second * math.sqrt(ROWS), right_full * math.sqrt(COLS), projection)
```

```python
import math

import jax
import jax.numpy as jnp
from jax import lax
from jax.sharding import PartitionSpec as P

EPSILON = 1e-05
CONTRACT_ROWS = (((0,), (0,)), ((), ()))
HIGHEST = lax.Precision.HIGHEST
COL_CORE, COL_X, COL_Y = (1, 2), (2, 4), (8, 4)
ROW_LOW, ROW_HIGH = (1, 4), (4, 4)


def unpack(words):
    shifts = 2 * jnp.arange(6, dtype=jnp.int32)
    parts = jnp.bitwise_and(jnp.right_shift(words[None, :, :], shifts[:, None, None]), 3)
    return (
        jnp.transpose(parts, (1, 0, 2))
        .reshape(words.shape[0], 6 * words.shape[1])
        .astype(jnp.float32)
    )


def place(axis, group):
    stride, size = group
    return lax.rem(lax.div(lax.axis_index(axis), stride), size)


def shift(block, axis, group, steps):
    stride, size = group
    pairs = []
    for index in range(lax.axis_size(axis)):
        mine = (index // stride) % size
        pairs.append((index, index + ((mine + steps) % size - mine) * stride))
    return lax.ppermute(block, axis, pairs)


def group_scatter(panel, axis, group):
    size = group[1]
    mine = place(axis, group)
    blocks = panel.reshape((size, panel.shape[0] // size) + panel.shape[1:])

    def block_at(index):
        return lax.dynamic_index_in_dim(blocks, lax.rem(index, size), 0, keepdims=False)

    arrived = [shift(block_at(mine + k), axis, group, k) for k in range(1, size)]
    total = block_at(mine)
    for block in arrived:
        total = total + block
    return total


def group_gather(block, axis, group):
    size = group[1]
    mine = place(axis, group)
    ordered = [block] + [shift(block, axis, group, size - j) for j in range(1, size)]
    ring = jnp.concatenate(ordered + ordered[:-1], axis=0)
    start = lax.rem(size - mine, size) * block.shape[0]
    return lax.dynamic_slice_in_dim(ring, start, size * block.shape[0], 0)


def grouped_sum(panel, axis, groups):
    for group in groups:
        panel = group_scatter(panel, axis, group)
    for group in reversed(groups):
        panel = group_gather(panel, axis, group)
    return panel


def exchanged_scatter(panel, axis):
    size = lax.axis_size(axis)
    blocks = panel.reshape((size, panel.shape[0] // size) + panel.shape[1:])
    arrived = lax.all_to_all(blocks, axis, split_axis=0, concat_axis=0, tiled=True)
    return jnp.sum(arrived.astype(jnp.float32), axis=0)


def inverse_factor(gram_sum):
    lower = jnp.linalg.cholesky(gram_sum)
    identity = jnp.eye(gram_sum.shape[0], dtype=jnp.float32)
    return lax.linalg.triangular_solve(lower, identity, left_side=True, lower=True)


def apply_factor(panel, inverse):
    return lax.dot_general(panel, inverse, (((1,), (1,)), ((), ())), precision=HIGHEST)


def local_gram(panel):
    return lax.dot_general(panel, panel, CONTRACT_ROWS, precision=HIGHEST)


def per_device(dosage_words, sample_weight, variant_weight, omega):
    dosage = unpack(dosage_words)
    rows_local, cols_local = dosage.shape
    rows_all = rows_local * lax.axis_size("row")
    cols_all = cols_local * lax.axis_size("col")
    sums = jnp.stack([jnp.sum(dosage, axis=0), jnp.sum(dosage * dosage, axis=0)])
    totals, squares = jnp.sum(lax.all_gather(sums, "row"), axis=0)
    column_mean = totals / rows_all
    column_scale = lax.rsqrt(squares / rows_all - column_mean * column_mean + EPSILON)
    matrix = (
        (dosage - column_mean) * column_scale * sample_weight[:, None] * variant_weight
    ).astype(jnp.bfloat16)

    sketch_part = jnp.dot(matrix, omega, preferred_element_type=jnp.float32)
    sketch = lax.all_gather(exchanged_scatter(sketch_part, "col"), "col", axis=0, tiled=True)
    gram = grouped_sum(local_gram(sketch), "row", (ROW_LOW, ROW_HIGH))
    first = apply_factor(sketch, inverse_factor(gram)).astype(jnp.bfloat16)

    back_part = lax.dot_general(
        matrix, first, CONTRACT_ROWS, preferred_element_type=jnp.float32
    ).astype(jnp.bfloat16)
    back_rows = exchanged_scatter(back_part, "row").astype(jnp.bfloat16)
    back = lax.all_gather(back_rows, "row", axis=0, tiled=True)

    both = jnp.concatenate(
        [
            jnp.dot(matrix, back, preferred_element_type=jnp.float32),
            lax.dot_general(back, back, CONTRACT_ROWS, preferred_element_type=jnp.float32),
        ],
        axis=0,
    )
    both = grouped_sum(both, "col", (COL_CORE, COL_X, COL_Y))
    inverse = inverse_factor(both[rows_local:])
    right_full = apply_factor(back.astype(jnp.float32), inverse)
    product = apply_factor(both[:rows_local], inverse)

    gram = lax.all_gather(
        exchanged_scatter(local_gram(product), "row"), "row", axis=0, tiled=True
    )
    inverse = inverse_factor(gram)
    second = apply_factor(product, inverse)
    own = rows_local // lax.axis_size("col")
    second_own = lax.dynamic_slice_in_dim(second, lax.axis_index("col") * own, own, 0)

    projection_part = lax.dot_general(
        second.astype(jnp.bfloat16), matrix, CONTRACT_ROWS, preferred_element_type=jnp.float32
    ).astype(jnp.bfloat16)
    projection = exchanged_scatter(projection_part, "row").T
    return (second_own * math.sqrt(rows_all), right_full * math.sqrt(cols_all), projection)


def solution(mesh):
    in_specs = (P("row", "col"), P("row"), P("col"), P("col", None))
    out_specs = (P(("row", "col"), None), P("col", None), P("col", "row"))
    return jax.shard_map(
        per_device, mesh=mesh, in_specs=in_specs, out_specs=out_specs, check_vma=False
    )
```

```python
import math

import jax
import jax.numpy as jnp
from jax import lax
from jax.experimental import pallas as pl
from jax.experimental.pallas import tpu as pltpu
from jax.sharding import PartitionSpec as P

EPSILON = 1e-05
PLACES = 6
CONTRACT_ROWS = (((0,), (0,)), ((), ()))
HIGHEST = lax.Precision.HIGHEST
VMEM_LIMIT = 32 * 1024 * 1024
BLOCK = 8


def exchange(blocks, axis):
    return lax.all_to_all(blocks, axis, split_axis=0, concat_axis=0, tiled=True)


def exchanged_scatter(panel, axis):
    size = lax.axis_size(axis)
    blocks = panel.reshape((size, panel.shape[0] // size) + panel.shape[1:])
    return jnp.sum(exchange(blocks, axis).astype(jnp.float32), axis=0)


def exchanged_gather(block, axis):
    size = lax.axis_size(axis)
    gathered = exchange(jnp.broadcast_to(block[None], (size,) + block.shape), axis)
    return gathered.reshape((size * block.shape[0],) + block.shape[1:])


def doubled_sum(panel, axis):
    size = lax.axis_size(axis)
    distance = 1
    while distance < size:
        pairs = [(index, index ^ distance) for index in range(size)]
        panel = panel + lax.ppermute(panel, axis, pairs)
        distance *= 2
    return panel


def pack(gram):
    return jnp.concatenate(
        [
            gram[0:32],
            jnp.concatenate([gram[96:128, 96:128], gram[32:64, 32:128]], axis=1),
            jnp.concatenate([gram[80:96, 64:128], gram[64:80, 64:128]], axis=1),
        ],
        axis=0,
    )


def unpack_upper(packed):
    zeros = jnp.zeros((32, 128), jnp.float32)
    return jnp.concatenate(
        [
            packed[0:32],
            jnp.concatenate([zeros[:, :32], packed[32:64, 32:128]], axis=1),
            jnp.concatenate([zeros[:16, :64], packed[64:80, 64:128]], axis=1),
            jnp.concatenate([zeros[:16, :64], packed[64:80, 0:64]], axis=1),
            jnp.concatenate([zeros[:, :96], packed[32:64, 0:32]], axis=1),
        ],
        axis=0,
    )


def symmetric(upper):
    rows = lax.broadcasted_iota(jnp.int32, upper.shape, 0)
    columns = lax.broadcasted_iota(jnp.int32, upper.shape, 1)
    return jnp.where(rows <= columns, upper, upper.T)


def inverse_factor_kernel(gram_ref, inverse_ref, work):
    size = gram_ref.shape[0]
    shape = (BLOCK, size)
    work[...] = gram_ref[...]
    lane = lax.broadcasted_iota(jnp.int32, shape, 1)
    sublane = lax.broadcasted_iota(jnp.int32, shape, 0)
    all_lanes = lax.broadcasted_iota(jnp.int32, (size, size), 1)

    def spread(rows):
        out = rows[0]
        for index in range(1, BLOCK):
            out = jnp.where(sublane == index, rows[index], out)
        return out

    def step(at, carry):
        base = pl.multiple_of(at * BLOCK, BLOCK)
        rows = work[pl.ds(base, BLOCK), :]
        turned = pltpu.roll(rows, lax.rem(size - base, size), 1)
        columns = [jnp.broadcast_to(turned[:, j : j + 1], shape) for j in range(BLOCK)]
        entry = {
            (i, j): jnp.broadcast_to(columns[i][j : j + 1, :], shape)
            for j in range(BLOCK)
            for i in range(j, BLOCK)
        }
        within = jnp.logical_and(lane >= base, lane < base + BLOCK)
        start = jnp.where(within, (lane - base == sublane).astype(jnp.float32), rows)
        done, pivots, reciprocals = [], [], []
        for j in range(BLOCK):
            pivots.append(entry[j, j])
            reciprocal = 1.0 / entry[j, j]
            reciprocals.append(reciprocal)
            factors = {i: entry[i, j] * reciprocal for i in range(j + 1, BLOCK)}
            for i in range(j + 1, BLOCK):
                for k in range(j + 1, i + 1):
                    entry[i, k] = entry[i, k] - factors[i] * entry[k, j]
            for i in range(j + 1, BLOCK):
                entry[i, j] = factors[i]
        for i in range(BLOCK):
            row = jnp.broadcast_to(start[i : i + 1, :], shape)
            for j in range(i):
                row = row - entry[i, j] * done[j]
            done.append(row)
        block = spread(done)
        inverse_ref[pl.ds(base, BLOCK), :] = jnp.where(
            lane < base + BLOCK, block, 0.0
        ) * lax.rsqrt(spread(pivots))
        factor = jnp.where(lane >= base + BLOCK, block * spread(reciprocals), 0.0)
        update = lax.dot_general(
            factor, block, CONTRACT_ROWS, precision=HIGHEST, preferred_element_type=jnp.float32
        )
        inside = jnp.logical_and(all_lanes >= base, all_lanes < base + BLOCK)
        work[...] = jnp.where(inside, 0.0, work[...]) - update
        return carry

    lax.fori_loop(0, size // BLOCK, step, 0)


def inverse_factor(gram_sum):
    vmem = pl.BlockSpec(memory_space=pltpu.VMEM)
    return pl.pallas_call(
        inverse_factor_kernel,
        out_shape=jax.ShapeDtypeStruct(gram_sum.shape, jnp.float32),
        in_specs=[vmem],
        out_specs=vmem,
        scratch_shapes=[pltpu.VMEM(gram_sum.shape, jnp.float32)],
        compiler_params=pltpu.CompilerParams(vmem_limit_bytes=VMEM_LIMIT),
        cost_estimate=pl.CostEstimate(
            flops=4 * 10**9, bytes_accessed=3 * 10**7, transcendentals=0
        ),
        name="inverse_factor",
    )(gram_sum)


def standardize_kernel(words_ref, weight_ref, mean_ref, scale_ref, matrix_ref):
    rows, width = words_ref.shape
    step = 64

    def chunk(at, carry):
        span = pl.ds(pl.multiple_of(at * step, step), step)
        words = words_ref[span, :]
        weight = jnp.broadcast_to(weight_ref[span, :], (step, width))
        for place in range(PLACES):
            across = slice(place * width, (place + 1) * width)
            dosage = jnp.bitwise_and(jnp.right_shift(words, 2 * place), 3).astype(jnp.float32)
            value = (dosage - mean_ref[:, across]) * scale_ref[:, across] * weight
            matrix_ref[span, across] = value.astype(jnp.bfloat16)
        return carry

    lax.fori_loop(0, rows // step, chunk, 0)


def standardize(words, sample_weight, column_mean, column_scale):
    rows, width = words.shape
    vmem = pl.BlockSpec(memory_space=pltpu.VMEM)
    return pl.pallas_call(
        standardize_kernel,
        out_shape=jax.ShapeDtypeStruct((rows, PLACES * width), jnp.bfloat16),
        in_specs=[vmem] * 4,
        out_specs=vmem,
        compiler_params=pltpu.CompilerParams(vmem_limit_bytes=VMEM_LIMIT),
        cost_estimate=pl.CostEstimate(
            flops=10**7, bytes_accessed=4 * 10**6, transcendentals=0
        ),
        name="standardize",
    )(words, sample_weight[:, None], column_mean[None, :], column_scale[None, :])


def apply_factor(panel, inverse):
    return lax.dot_general(panel, inverse, (((1,), (1,)), ((), ())), precision=HIGHEST)


def local_gram(panel):
    return lax.dot_general(panel, panel, CONTRACT_ROWS, precision=HIGHEST)


def per_device(dosage_words, sample_weight, variant_weight, omega):
    rows_local, width = dosage_words.shape
    rows_all = rows_local * lax.axis_size("row")
    cols_all = PLACES * width * lax.axis_size("col")
    dosage = [
        jnp.bitwise_and(jnp.right_shift(dosage_words, 2 * place), 3).astype(jnp.float32)
        for place in range(PLACES)
    ]
    sums = jnp.concatenate(
        [jnp.sum(part, axis=0) for part in dosage]
        + [jnp.sum(part * part, axis=0) for part in dosage]
    )
    totals, squares = doubled_sum(sums.reshape(-1, 128), "row").reshape(2, PLACES * width)
    column_mean = totals / rows_all
    column_scale = lax.rsqrt(squares / rows_all - column_mean * column_mean + EPSILON)
    matrix = standardize(
        dosage_words, sample_weight, column_mean, column_scale * variant_weight
    )

    sketch_part = jnp.dot(matrix, omega, preferred_element_type=jnp.float32)
    sketch = exchanged_gather(exchanged_scatter(sketch_part, "col"), "col")
    gram = unpack_upper(doubled_sum(pack(local_gram(sketch)), "row"))
    first = apply_factor(sketch, inverse_factor(gram)).astype(jnp.bfloat16)

    back_part = lax.dot_general(
        matrix, first, CONTRACT_ROWS, preferred_element_type=jnp.float32
    ).astype(jnp.bfloat16)
    back = exchanged_gather(exchanged_scatter(back_part, "row").astype(jnp.bfloat16), "row")

    both = jnp.concatenate(
        [
            jnp.dot(matrix, back, preferred_element_type=jnp.float32),
            lax.dot_general(back, back, CONTRACT_ROWS, preferred_element_type=jnp.float32),
        ],
        axis=0,
    )
    both = exchanged_gather(exchanged_scatter(both, "col"), "col")
    product = both[:rows_local]

    gathered = exchanged_gather(pack(local_gram(product))[None], "row")
    inverse = inverse_factor(both[rows_local:])
    right_full = apply_factor(back.astype(jnp.float32), inverse)
    product = apply_factor(product, inverse)
    gram = symmetric(unpack_upper(jnp.sum(gathered, axis=0)))
    gram = apply_factor(jnp.dot(inverse, gram, precision=HIGHEST), inverse)
    second = apply_factor(product, inverse_factor(gram))
    own = rows_local // lax.axis_size("col")
    second_own = lax.dynamic_slice_in_dim(second, lax.axis_index("col") * own, own, 0)

    projection_part = lax.dot_general(
        second.astype(jnp.bfloat16), matrix, CONTRACT_ROWS, preferred_element_type=jnp.float32
    ).astype(jnp.bfloat16)
    projection = exchanged_scatter(projection_part, "row").T
    return (second_own * math.sqrt(rows_all), right_full * math.sqrt(cols_all), projection)


def solution(mesh):
    in_specs = (P("row", "col"), P("row"), P("col"), P("col", None))
    out_specs = (P(("row", "col"), None), P("col", None), P("col", "row"))
    return jax.shard_map(
        per_device, mesh=mesh, in_specs=in_specs, out_specs=out_specs, check_vma=False
    )
```

```python
import math

import jax
import jax.numpy as jnp
from jax import lax
from jax.experimental import pallas as pl
from jax.experimental.pallas import tpu as pltpu
from jax.sharding import PartitionSpec as P

EPSILON = 1e-05
PLACES = 6
RANK = 128
CONTRACT_ROWS = (((0,), (0,)), ((), ()))
HIGHEST = lax.Precision.HIGHEST
VMEM_LIMIT = 32 * 1024 * 1024
BLOCK = 8


def exchange(blocks, axis):
    return lax.all_to_all(blocks, axis, split_axis=0, concat_axis=0, tiled=True)


def exchanged_gather(block, axis):
    size = lax.axis_size(axis)
    return exchange(jnp.broadcast_to(block[None], (size,) + block.shape), axis)


def halves(values, count):
    terms = []
    for index in range(count):
        term = lax.reduce_precision(values, exponent_bits=8, mantissa_bits=7)
        values = values - term
        terms.append(term.astype(jnp.bfloat16))
    return terms


def pack(gram):
    return jnp.concatenate(
        [
            gram[0:32],
            jnp.concatenate([gram[96:128, 96:128], gram[32:64, 32:128]], axis=1),
            jnp.concatenate([gram[80:96, 64:128], gram[64:80, 64:128]], axis=1),
        ],
        axis=0,
    )


def unpack_upper(packed):
    zeros = jnp.zeros((32, 128), jnp.float32)
    return jnp.concatenate(
        [
            packed[0:32],
            jnp.concatenate([zeros[:, :32], packed[32:64, 32:128]], axis=1),
            jnp.concatenate([zeros[:16, :64], packed[64:80, 64:128]], axis=1),
            jnp.concatenate([zeros[:16, :64], packed[64:80, 0:64]], axis=1),
            jnp.concatenate([zeros[:, :96], packed[32:64, 0:32]], axis=1),
        ],
        axis=0,
    )


def symmetric(upper):
    rows = lax.broadcasted_iota(jnp.int32, upper.shape, 0)
    columns = lax.broadcasted_iota(jnp.int32, upper.shape, 1)
    return jnp.where(rows <= columns, upper, upper.T)


def inverse_factor_kernel(gram_ref, inverse_ref, work):
    size = gram_ref.shape[0]
    shape = (BLOCK, size)
    work[...] = gram_ref[...]
    lane = lax.broadcasted_iota(jnp.int32, shape, 1)
    sublane = lax.broadcasted_iota(jnp.int32, shape, 0)
    all_lanes = lax.broadcasted_iota(jnp.int32, (size, size), 1)

    def spread(rows):
        out = rows[0]
        for index in range(1, BLOCK):
            out = jnp.where(sublane == index, rows[index], out)
        return out

    def step(at, carry):
        base = pl.multiple_of(at * BLOCK, BLOCK)
        rows = work[pl.ds(base, BLOCK), :]
        turned = pltpu.roll(rows, lax.rem(size - base, size), 1)
        columns = [jnp.broadcast_to(turned[:, j : j + 1], shape) for j in range(BLOCK)]
        entry = {
            (i, j): jnp.broadcast_to(columns[i][j : j + 1, :], shape)
            for j in range(BLOCK)
            for i in range(j, BLOCK)
        }
        within = jnp.logical_and(lane >= base, lane < base + BLOCK)
        start = jnp.where(within, (lane - base == sublane).astype(jnp.float32), rows)
        done, pivots, reciprocals = [], [], []
        for j in range(BLOCK):
            pivots.append(entry[j, j])
            reciprocal = 1.0 / entry[j, j]
            reciprocals.append(reciprocal)
            factors = {i: entry[i, j] * reciprocal for i in range(j + 1, BLOCK)}
            for i in range(j + 1, BLOCK):
                for k in range(j + 1, i + 1):
                    entry[i, k] = entry[i, k] - factors[i] * entry[k, j]
            for i in range(j + 1, BLOCK):
                entry[i, j] = factors[i]
        for i in range(BLOCK):
            row = jnp.broadcast_to(start[i : i + 1, :], shape)
            for j in range(i):
                row = row - entry[i, j] * done[j]
            done.append(row)
        block = spread(done)
        inverse_ref[pl.ds(base, BLOCK), :] = jnp.where(
            lane < base + BLOCK, block, 0.0
        ) * lax.rsqrt(spread(pivots))
        factor = jnp.where(lane >= base + BLOCK, block * spread(reciprocals), 0.0)
        update = lax.dot_general(
            factor, block, CONTRACT_ROWS, precision=HIGHEST, preferred_element_type=jnp.float32
        )
        inside = jnp.logical_and(all_lanes >= base, all_lanes < base + BLOCK)
        work[...] = jnp.where(inside, 0.0, work[...]) - update
        return carry

    lax.fori_loop(0, size // BLOCK, step, 0)


def inverse_factor(gram_sum):
    vmem = pl.BlockSpec(memory_space=pltpu.VMEM)
    return pl.pallas_call(
        inverse_factor_kernel,
        out_shape=jax.ShapeDtypeStruct(gram_sum.shape, jnp.float32),
        in_specs=[vmem],
        out_specs=vmem,
        scratch_shapes=[pltpu.VMEM(gram_sum.shape, jnp.float32)],
        compiler_params=pltpu.CompilerParams(vmem_limit_bytes=VMEM_LIMIT),
        cost_estimate=pl.CostEstimate(
            flops=4 * 10**9, bytes_accessed=3 * 10**7, transcendentals=0
        ),
        name="inverse_factor",
    )(gram_sum)


def standardize_kernel(words_ref, weight_ref, mean_ref, scale_ref, matrix_ref):
    rows, width = words_ref.shape
    step = 64

    def chunk(at, carry):
        span = pl.ds(pl.multiple_of(at * step, step), step)
        words = words_ref[span, :]
        weight = jnp.broadcast_to(weight_ref[span, :], (step, width))
        for place in range(PLACES):
            across = slice(place * width, (place + 1) * width)
            dosage = jnp.bitwise_and(jnp.right_shift(words, 2 * place), 3).astype(jnp.float32)
            value = (dosage - mean_ref[:, across]) * scale_ref[:, across] * weight
            matrix_ref[span, across] = value.astype(jnp.bfloat16)
        return carry

    lax.fori_loop(0, rows // step, chunk, 0)


def standardize(words, sample_weight, column_mean, column_scale):
    rows, width = words.shape
    vmem = pl.BlockSpec(memory_space=pltpu.VMEM)
    return pl.pallas_call(
        standardize_kernel,
        out_shape=jax.ShapeDtypeStruct((rows, PLACES * width), jnp.bfloat16),
        in_specs=[vmem] * 4,
        out_specs=vmem,
        compiler_params=pltpu.CompilerParams(vmem_limit_bytes=VMEM_LIMIT),
        cost_estimate=pl.CostEstimate(
            flops=10**7, bytes_accessed=4 * 10**6, transcendentals=0
        ),
        name="standardize",
    )(words, sample_weight[:, None], column_mean[None, :], column_scale[None, :])


def apply_factor(panel, inverse):
    return lax.dot_general(panel, inverse, (((1,), (1,)), ((), ())), precision=HIGHEST)


def congruent(gram, factor):
    return apply_factor(jnp.dot(factor, gram, precision=HIGHEST), factor)


def local_gram(panel):
    return lax.dot_general(panel, panel, CONTRACT_ROWS, precision=HIGHEST)


def per_device(dosage_words, sample_weight, variant_weight, omega):
    rows_local, width = dosage_words.shape
    rows_all = rows_local * lax.axis_size("row")
    cols_all = PLACES * width * lax.axis_size("col")
    dosage = [
        jnp.bitwise_and(jnp.right_shift(dosage_words, 2 * place), 3).astype(jnp.float32)
        for place in range(PLACES)
    ]
    sums = jnp.concatenate(
        [jnp.sum(part, axis=0) for part in dosage]
        + [jnp.sum(part * part, axis=0) for part in dosage]
    )
    sums = jnp.sum(exchanged_gather(sums.reshape(-1, 128), "row"), axis=0)
    totals, squares = sums.reshape(2, PLACES * width)
    column_mean = totals / rows_all
    column_scale = lax.rsqrt(squares / rows_all - column_mean * column_mean + EPSILON)
    matrix = standardize(
        dosage_words, sample_weight, column_mean, column_scale * variant_weight
    )
    n_row, n_col = lax.axis_size("row"), lax.axis_size("col")
    col = lax.axis_index("col")
    own, part = rows_local // n_col, RANK // n_col
    chunk = PLACES * width // n_row

    sketch_part = jnp.dot(matrix, omega, preferred_element_type=jnp.float32)
    sketch_own = jnp.sum(exchange(sketch_part.reshape(n_col, own, RANK), "col"), axis=0)
    sketch = exchanged_gather(sketch_own, "col").reshape(rows_local, RANK)

    gram_share = lax.dynamic_slice_in_dim(local_gram(sketch), col * part, part, 0)
    sketch_terms = jnp.concatenate(halves(sketch, 2), axis=1)
    back_terms = lax.dot_general(
        matrix, sketch_terms, CONTRACT_ROWS, preferred_element_type=jnp.float32
    )
    back_part = (back_terms[:, :RANK] + back_terms[:, RANK:]).astype(jnp.bfloat16)
    share_terms = jnp.concatenate(
        halves(gram_share, 3) + [jnp.zeros((part, RANK), jnp.bfloat16)], axis=0
    )
    arrived = exchange(
        jnp.concatenate(
            [
                back_part.reshape(n_row, chunk, RANK),
                jnp.broadcast_to(share_terms[None], (n_row,) + share_terms.shape),
            ],
            axis=1,
        ),
        "row",
    )
    arrived = jnp.sum(arrived.astype(jnp.float32), axis=0)
    back_own = arrived[:chunk].astype(jnp.bfloat16)
    gram_share = jnp.sum(arrived[chunk:].reshape(4, part, RANK), axis=0)
    back = exchanged_gather(back_own, "row").reshape(n_row * chunk, RANK)

    product_part = jnp.dot(matrix, back, preferred_element_type=jnp.float32)
    back_gram = lax.dot_general(back, back, CONTRACT_ROWS, preferred_element_type=jnp.float32)
    back_gram = lax.optimization_barrier(back_gram)
    arrived = exchange(
        jnp.concatenate(
            [
                product_part.reshape(n_col, own, RANK),
                back_gram.reshape(n_col, part, RANK),
                jnp.broadcast_to(gram_share[None], (n_col, part, RANK)),
            ],
            axis=1,
        ),
        "col",
    )
    summed = jnp.sum(arrived[:, : own + part], axis=0)
    sketch_factor = inverse_factor(arrived[:, own + part :].reshape(RANK, RANK))
    gathered = exchanged_gather(
        jnp.concatenate([summed, jnp.zeros((part, RANK), jnp.float32)], axis=0), "col"
    )
    gathered, sketch_factor = lax.optimization_barrier((gathered, sketch_factor))
    product = gathered[:, :own].reshape(rows_local, RANK)
    back_gram = gathered[:, own : own + part].reshape(RANK, RANK)

    packed = pack(local_gram(product))
    half = packed.shape[0] // 2
    core = lax.rem(col, 2)
    gathered = exchanged_gather(
        lax.dynamic_slice_in_dim(packed, core * half, half, 0), "row"
    )
    back_factor = inverse_factor(congruent(back_gram, sketch_factor))
    factor = jnp.dot(back_factor, sketch_factor, precision=HIGHEST)
    right_full = apply_factor(back.astype(jnp.float32), factor)
    product = apply_factor(product, factor)
    gathered, product = lax.optimization_barrier((gathered, product))
    packed = jnp.sum(gathered, axis=0)
    other = lax.ppermute(packed, "col", [(index, index ^ 1) for index in range(n_col)])
    packed = jnp.where(
        core == 0,
        jnp.concatenate([packed, other], axis=0),
        jnp.concatenate([other, packed], axis=0),
    )
    gram = congruent(symmetric(unpack_upper(packed)), factor)
    second = apply_factor(product, inverse_factor(gram))
    second_own = lax.dynamic_slice_in_dim(second, col * own, own, 0)

    projection_part = lax.dot_general(
        second.astype(jnp.bfloat16), matrix, CONTRACT_ROWS, preferred_element_type=jnp.float32
    ).astype(jnp.bfloat16)
    arrived = exchange(projection_part.reshape(n_row, RANK // n_row, -1), "row")
    projection = jnp.sum(arrived.astype(jnp.float32), axis=0).T
    return (second_own * math.sqrt(rows_all), right_full * math.sqrt(cols_all), projection)


def solution(mesh):
    in_specs = (P("row", "col"), P("row"), P("col"), P("col", None))
    out_specs = (P(("row", "col"), None), P("col", None), P("col", "row"))
    return jax.shard_map(
        per_device, mesh=mesh, in_specs=in_specs, out_specs=out_specs, check_vma=False
    )
```

```python
import math

import jax
import jax.numpy as jnp
from jax import lax
from jax.experimental import pallas as pl
from jax.experimental.pallas import tpu as pltpu
from jax.sharding import PartitionSpec as P

EPSILON = 1e-05
PLACES = 6
RANK = 128
COUNT_ROWS = 16
PACKED_ROWS = 80
CONTRACT_ROWS = (((0,), (0,)), ((), ()))
HIGHEST = lax.Precision.HIGHEST
VMEM_LIMIT = 32 * 1024 * 1024
BLOCK = 8


def exchange(blocks, axis):
    return lax.all_to_all(blocks, axis, split_axis=0, concat_axis=0, tiled=True)


def halves(values, count):
    terms = []
    for index in range(count):
        term = lax.reduce_precision(values, exponent_bits=8, mantissa_bits=7)
        values = values - term
        terms.append(term.astype(jnp.bfloat16))
    return terms


def pack(gram):
    return jnp.concatenate(
        [
            gram[0:32],
            jnp.concatenate([gram[96:128, 96:128], gram[32:64, 32:128]], axis=1),
            jnp.concatenate([gram[80:96, 64:128], gram[64:80, 64:128]], axis=1),
        ],
        axis=0,
    )


def unpack_upper(packed):
    zeros = jnp.zeros((32, 128), jnp.float32)
    return jnp.concatenate(
        [
            packed[0:32],
            jnp.concatenate([zeros[:, :32], packed[32:64, 32:128]], axis=1),
            jnp.concatenate([zeros[:16, :64], packed[64:80, 64:128]], axis=1),
            jnp.concatenate([zeros[:16, :64], packed[64:80, 0:64]], axis=1),
            jnp.concatenate([zeros[:, :96], packed[32:64, 0:32]], axis=1),
        ],
        axis=0,
    )


def symmetric(upper):
    rows = lax.broadcasted_iota(jnp.int32, upper.shape, 0)
    columns = lax.broadcasted_iota(jnp.int32, upper.shape, 1)
    return jnp.where(rows <= columns, upper, upper.T)


def inverse_factor_kernel(gram_ref, inverse_ref, work):
    size = gram_ref.shape[0]
    shape = (BLOCK, size)
    work[...] = gram_ref[...]
    lane = lax.broadcasted_iota(jnp.int32, shape, 1)
    sublane = lax.broadcasted_iota(jnp.int32, shape, 0)
    all_lanes = lax.broadcasted_iota(jnp.int32, (size, size), 1)

    def spread(rows):
        out = rows[0]
        for index in range(1, BLOCK):
            out = jnp.where(sublane == index, rows[index], out)
        return out

    def step(at, carry):
        base = pl.multiple_of(at * BLOCK, BLOCK)
        rows = work[pl.ds(base, BLOCK), :]
        turned = pltpu.roll(rows, lax.rem(size - base, size), 1)
        columns = [jnp.broadcast_to(turned[:, j : j + 1], shape) for j in range(BLOCK)]
        entry = {
            (i, j): jnp.broadcast_to(columns[i][j : j + 1, :], shape)
            for j in range(BLOCK)
            for i in range(j, BLOCK)
        }
        within = jnp.logical_and(lane >= base, lane < base + BLOCK)
        start = jnp.where(within, (lane - base == sublane).astype(jnp.float32), rows)
        done, pivots, reciprocals = [], [], []
        for j in range(BLOCK):
            pivots.append(entry[j, j])
            reciprocal = 1.0 / entry[j, j]
            reciprocals.append(reciprocal)
            factors = {i: entry[i, j] * reciprocal for i in range(j + 1, BLOCK)}
            for i in range(j + 1, BLOCK):
                for k in range(j + 1, i + 1):
                    entry[i, k] = entry[i, k] - factors[i] * entry[k, j]
            for i in range(j + 1, BLOCK):
                entry[i, j] = factors[i]
        for i in range(BLOCK):
            row = jnp.broadcast_to(start[i : i + 1, :], shape)
            for j in range(i):
                row = row - entry[i, j] * done[j]
            done.append(row)
        block = spread(done)
        inverse_ref[pl.ds(base, BLOCK), :] = jnp.where(
            lane < base + BLOCK, block, 0.0
        ) * lax.rsqrt(spread(pivots))
        factor = jnp.where(lane >= base + BLOCK, block * spread(reciprocals), 0.0)
        update = lax.dot_general(
            factor, block, CONTRACT_ROWS, precision=HIGHEST, preferred_element_type=jnp.float32
        )
        inside = jnp.logical_and(all_lanes >= base, all_lanes < base + BLOCK)
        work[...] = jnp.where(inside, 0.0, work[...]) - update
        return carry

    lax.fori_loop(0, size // BLOCK, step, 0)


def inverse_factor(gram_sum):
    return call(
        inverse_factor_kernel,
        "inverse_factor",
        jax.ShapeDtypeStruct(gram_sum.shape, jnp.float32),
        (gram_sum,),
        scratch=[pltpu.VMEM(gram_sum.shape, jnp.float32)],
        flops=4 * 10**9,
        moved=3 * 10**7,
    )


def call(kernel, name, shapes, operands, scratch=(), flops=10**7, moved=4 * 10**6):
    vmem = pl.BlockSpec(memory_space=pltpu.VMEM)
    smem = pl.BlockSpec(memory_space=pltpu.SMEM)
    return pl.pallas_call(
        kernel,
        out_shape=shapes,
        in_specs=[smem if operand.ndim == 1 else vmem for operand in operands],
        out_specs=jax.tree.map(lambda _: vmem, shapes),
        scratch_shapes=scratch,
        compiler_params=pltpu.CompilerParams(vmem_limit_bytes=VMEM_LIMIT),
        cost_estimate=pl.CostEstimate(flops=flops, bytes_accessed=moved, transcendentals=0),
        name=name,
    )(*operands)


def count_kernel(words_ref, spread_ref):
    rows, width = words_ref.shape
    step = 64

    def chunk(at, totals):
        words = words_ref[pl.ds(pl.multiple_of(at * step, step), step), :]
        bits = [
            jnp.bitwise_and(jnp.right_shift(words, 2 * place + bit), 1)
            for bit in range(2)
            for place in range(PLACES)
        ]
        return tuple(
            total + jnp.sum(bit.reshape(step // 8, 8, width), axis=0)
            for total, bit in zip(totals, bits)
        )

    zeros = jnp.zeros((8, width), jnp.int32)
    totals = lax.fori_loop(0, rows // step, chunk, (zeros,) * (2 * PLACES))
    shape = (COUNT_ROWS, width)
    sublane = lax.broadcasted_iota(jnp.int32, shape, 0)
    out = jnp.zeros(shape, jnp.float32)
    for index, total in enumerate(totals):
        count = jnp.sum(total.astype(jnp.float32), axis=0, keepdims=True) - rows / 2
        out = jnp.where(sublane == index, jnp.broadcast_to(count, shape), out)
    out = out.astype(jnp.bfloat16)
    for index in range(spread_ref.shape[0]):
        spread_ref[index] = out


def standardize_kernel(counts_ref, words_ref, weight_ref, variant_ref, matrix_ref):
    rows, width = words_ref.shape
    rows_all = rows * counts_ref.shape[0]
    counts = counts_ref[0].astype(jnp.float32)
    for index in range(1, counts_ref.shape[0]):
        counts = counts + counts_ref[index].astype(jnp.float32)
    counts = counts + rows_all / 2
    ones, twos = counts[:PLACES], counts[PLACES : 2 * PLACES]
    mean = (ones + 2 * twos) / rows_all
    scale = lax.rsqrt((ones + 4 * twos) / rows_all - mean * mean + EPSILON) * variant_ref[...]
    step = 64

    def chunk(at, carry):
        span = pl.ds(pl.multiple_of(at * step, step), step)
        words = words_ref[span, :]
        weight = jnp.broadcast_to(weight_ref[span, :], (step, width))
        for place in range(PLACES):
            across = slice(place * width, (place + 1) * width)
            dosage = jnp.bitwise_and(jnp.right_shift(words, 2 * place), 3).astype(jnp.float32)
            value = (dosage - mean[place : place + 1]) * scale[place : place + 1] * weight
            matrix_ref[span, across] = value.astype(jnp.bfloat16)
        return carry

    lax.fori_loop(0, rows // step, chunk, 0)


def sum_spread_kernel(*refs):
    blocks_ref, spread_ref = refs[0], refs[-1]
    total = blocks_ref[0].astype(jnp.float32)
    for index in range(1, blocks_ref.shape[0]):
        total = total + blocks_ref[index].astype(jnp.float32)
    total = total.astype(spread_ref.dtype)
    for index in range(spread_ref.shape[0]):
        spread_ref[index, : total.shape[0]] = total
    if len(refs) == 3:
        tail = refs[1][...]
        for index in range(spread_ref.shape[0]):
            spread_ref[index, total.shape[0] :] = tail


def sum_spread(blocks, *tail):
    count, rows, width = blocks.shape
    rows += sum(part.shape[0] for part in tail)
    shape = jax.ShapeDtypeStruct((count, rows, width), blocks.dtype)
    return call(sum_spread_kernel, "sum_spread", shape, (blocks, *tail))


def product_kernel(core_ref, gathered_ref, product_ref, spread_ref, packed):
    count = gathered_ref.shape[0]
    own = product_ref.shape[0] // count
    for index in range(count):
        product_ref[index * own : (index + 1) * own] = gathered_ref[index, :own]
    product = product_ref[...]
    gram = lax.dot_general(
        product, product, CONTRACT_ROWS, precision=HIGHEST, preferred_element_type=jnp.float32
    )
    packed[...] = pack(gram)
    half = packed.shape[0] // 2
    share = packed[pl.ds(pl.multiple_of(core_ref[0] * half, 8), half), :]
    for index in range(spread_ref.shape[0]):
        spread_ref[index] = share


def apply_factor(panel, inverse):
    return lax.dot_general(panel, inverse, (((1,), (1,)), ((), ())), precision=HIGHEST)


def congruent(gram, factor):
    return apply_factor(jnp.dot(factor, gram, precision=HIGHEST), factor)


def local_gram(panel):
    return lax.dot_general(panel, panel, CONTRACT_ROWS, precision=HIGHEST)


def per_device(dosage_words, sample_weight, variant_weight, omega):
    rows_local, width = dosage_words.shape
    rows_all = rows_local * lax.axis_size("row")
    cols_all = PLACES * width * lax.axis_size("col")
    n_row, n_col = lax.axis_size("row"), lax.axis_size("col")
    counts = call(
        count_kernel,
        "count",
        jax.ShapeDtypeStruct((n_row, COUNT_ROWS, width), jnp.bfloat16),
        (dosage_words,),
    )
    matrix = call(
        standardize_kernel,
        "standardize",
        jax.ShapeDtypeStruct((rows_local, PLACES * width), jnp.bfloat16),
        (
            exchange(counts, "row"),
            dosage_words,
            sample_weight[:, None],
            variant_weight.reshape(PLACES, width),
        ),
    )
    col = lax.axis_index("col")
    own, part = rows_local // n_col, RANK // n_col
    chunk = PLACES * width // n_row

    sketch_part = jnp.dot(matrix, omega, preferred_element_type=jnp.float32)
    arrived = exchange(sketch_part.reshape(n_col, own, RANK), "col")
    sketch = exchange(sum_spread(arrived), "col").reshape(rows_local, RANK)

    sketch_terms = jnp.concatenate(halves(sketch, 2), axis=1)
    back_terms = lax.dot_general(
        matrix, sketch_terms, CONTRACT_ROWS, preferred_element_type=jnp.float32
    )
    back_part = (back_terms[:, :RANK] + back_terms[:, RANK:]).astype(jnp.bfloat16)
    arrived = exchange(back_part.reshape(n_row, chunk, RANK), "row")
    gram_share = lax.dynamic_slice_in_dim(local_gram(sketch), col * part, part, 0)
    share_terms = jnp.concatenate(
        halves(gram_share, 3) + [jnp.zeros((part, RANK), jnp.bfloat16)], axis=0
    )
    arrived, share_terms = lax.optimization_barrier((arrived, share_terms))
    gathered = exchange(sum_spread(arrived, share_terms), "row")
    back = gathered[:, :chunk].reshape(n_row * chunk, RANK)
    gram_share = jnp.sum(
        gathered[:, chunk:].astype(jnp.float32).reshape(4 * n_row, part, RANK), axis=0
    )

    product_part = jnp.dot(matrix, back, preferred_element_type=jnp.float32)
    back_gram = lax.dot_general(back, back, CONTRACT_ROWS, preferred_element_type=jnp.float32)
    back_gram = lax.optimization_barrier(back_gram)
    arrived = exchange(
        jnp.concatenate(
            [
                product_part.reshape(n_col, own, RANK),
                back_gram.reshape(n_col, part, RANK),
                jnp.broadcast_to(gram_share[None], (n_col, part, RANK)),
            ],
            axis=1,
        ),
        "col",
    )
    sketch_factor = inverse_factor(arrived[:, own + part :].reshape(RANK, RANK))
    gathered = exchange(sum_spread(arrived), "col")
    gathered, sketch_factor = lax.optimization_barrier((gathered, sketch_factor))
    back_gram = gathered[:, own : own + part].reshape(RANK, RANK)

    core = lax.rem(col, 2)
    product, spread = call(
        product_kernel,
        "product",
        (
            jax.ShapeDtypeStruct((rows_local, RANK), jnp.float32),
            jax.ShapeDtypeStruct((n_row, PACKED_ROWS // 2, RANK), jnp.float32),
        ),
        (core.reshape(1), gathered),
        scratch=[pltpu.VMEM((PACKED_ROWS, RANK), jnp.float32)],
    )
    gathered = exchange(spread, "row")
    back_factor = inverse_factor(congruent(back_gram, sketch_factor))
    factor = jnp.dot(back_factor, sketch_factor, precision=HIGHEST)
    right_full = apply_factor(back.astype(jnp.float32), factor)
    product = apply_factor(product, factor)
    gathered, product = lax.optimization_barrier((gathered, product))
    packed = jnp.sum(gathered, axis=0)
    other = lax.ppermute(packed, "col", [(index, index ^ 1) for index in range(n_col)])
    packed = jnp.where(
        core == 0,
        jnp.concatenate([packed, other], axis=0),
        jnp.concatenate([other, packed], axis=0),
    )
    gram = congruent(symmetric(unpack_upper(packed)), factor)
    second = apply_factor(product, inverse_factor(gram))
    second_own = lax.dynamic_slice_in_dim(second, col * own, own, 0)

    projection_part = lax.dot_general(
        second.astype(jnp.bfloat16), matrix, CONTRACT_ROWS, preferred_element_type=jnp.float32
    ).astype(jnp.bfloat16)
    arrived = exchange(projection_part.reshape(n_row, RANK // n_row, -1), "row")
    projection = jnp.sum(arrived.astype(jnp.float32), axis=0).T
    return (second_own * math.sqrt(rows_all), right_full * math.sqrt(cols_all), projection)


def solution(mesh):
    in_specs = (P("row", "col"), P("row"), P("col"), P("col", None))
    out_specs = (P(("row", "col"), None), P("col", None), P("col", "row"))
    return jax.shard_map(
        per_device, mesh=mesh, in_specs=in_specs, out_specs=out_specs, check_vma=False
    )
```

```python
import math

import jax
import jax.numpy as jnp
from jax import lax
from jax.experimental import pallas as pl
from jax.experimental.pallas import tpu as pltpu
from jax.sharding import PartitionSpec as P

EPSILON = 1e-05
PLACES = 6
RANK = 128
COUNT_ROWS = 16
PACKED_ROWS = 80
CONTRACT_ROWS = (((0,), (0,)), ((), ()))
HIGHEST = lax.Precision.HIGHEST
VMEM_LIMIT = 32 * 1024 * 1024
BLOCK = 16
SUBLANES = 8


def exchange(blocks, axis):
    return lax.all_to_all(blocks, axis, split_axis=0, concat_axis=0, tiled=True)


def halves(values, count):
    terms = []
    for index in range(count):
        term = lax.reduce_precision(values, exponent_bits=8, mantissa_bits=7)
        values = values - term
        terms.append(term.astype(jnp.bfloat16))
    return terms


def pack(gram):
    return jnp.concatenate(
        [
            gram[0:32],
            jnp.concatenate([gram[96:128, 96:128], gram[32:64, 32:128]], axis=1),
            jnp.concatenate([gram[80:96, 64:128], gram[64:80, 64:128]], axis=1),
        ],
        axis=0,
    )


def unpack_upper(packed):
    zeros = jnp.zeros((32, 128), jnp.float32)
    return jnp.concatenate(
        [
            packed[0:32],
            jnp.concatenate([zeros[:, :32], packed[32:64, 32:128]], axis=1),
            jnp.concatenate([zeros[:16, :64], packed[64:80, 64:128]], axis=1),
            jnp.concatenate([zeros[:16, :64], packed[64:80, 0:64]], axis=1),
            jnp.concatenate([zeros[:, :96], packed[32:64, 0:32]], axis=1),
        ],
        axis=0,
    )


def symmetric(upper):
    rows = lax.broadcasted_iota(jnp.int32, upper.shape, 0)
    columns = lax.broadcasted_iota(jnp.int32, upper.shape, 1)
    return jnp.where(rows <= columns, upper, upper.T)


def inverse_factor_kernel(gram_ref, inverse_ref, work):
    size = gram_ref.shape[0]
    whole, tile = (BLOCK, size), (SUBLANES, size)
    work[...] = gram_ref[...]
    lane = lax.broadcasted_iota(jnp.int32, whole, 1)
    row_at = lax.broadcasted_iota(jnp.int32, whole, 0)
    sublane = lax.broadcasted_iota(jnp.int32, tile, 0)
    all_lanes = lax.broadcasted_iota(jnp.int32, (size, size), 1)

    def spread(rows):
        tiles = []
        for first in range(0, BLOCK, SUBLANES):
            out = rows[first]
            for index in range(1, SUBLANES):
                out = jnp.where(sublane == index, rows[first + index], out)
            tiles.append(out)
        return jnp.concatenate(tiles, axis=0)

    def step(at, carry):
        base = pl.multiple_of(at * BLOCK, BLOCK)
        rows = work[pl.ds(base, BLOCK), :]
        turned = pltpu.roll(rows, lax.rem(size - base, size), 1)
        columns = [jnp.broadcast_to(turned[:, j : j + 1], whole) for j in range(BLOCK)]
        entry = {
            (i, j): jnp.broadcast_to(columns[i][j : j + 1, :], tile)
            for j in range(BLOCK)
            for i in range(j, BLOCK)
        }
        within = jnp.logical_and(lane >= base, lane < base + BLOCK)
        start = jnp.where(within, (lane - base == row_at).astype(jnp.float32), rows)
        done, pivots, reciprocals = [], [], []
        for j in range(BLOCK):
            row = jnp.broadcast_to(start[j : j + 1, :], tile)
            for k in range(j):
                row = row - entry[j, k] * done[k]
            done.append(row)
            pivots.append(entry[j, j])
            reciprocal = 1.0 / entry[j, j]
            reciprocals.append(reciprocal)
            factors = {i: entry[i, j] * reciprocal for i in range(j + 1, BLOCK)}
            for i in range(j + 1, BLOCK):
                for k in range(j + 1, i + 1):
                    entry[i, k] = entry[i, k] - factors[i] * entry[k, j]
            for i in range(j + 1, BLOCK):
                entry[i, j] = factors[i]
        block = spread(done)
        inverse_ref[pl.ds(base, BLOCK), :] = jnp.where(
            lane < base + BLOCK, block, 0.0
        ) * lax.rsqrt(spread(pivots))
        factor = jnp.where(lane >= base + BLOCK, block * spread(reciprocals), 0.0)
        update = lax.dot_general(
            factor, block, CONTRACT_ROWS, precision=HIGHEST, preferred_element_type=jnp.float32
        )
        inside = jnp.logical_and(all_lanes >= base, all_lanes < base + BLOCK)
        work[...] = jnp.where(inside, 0.0, work[...]) - update
        return carry

    lax.fori_loop(0, size // BLOCK, step, 0)


def inverse_factor(gram_sum):
    return call(
        inverse_factor_kernel,
        "inverse_factor",
        jax.ShapeDtypeStruct(gram_sum.shape, jnp.float32),
        (gram_sum,),
        scratch=[pltpu.VMEM(gram_sum.shape, jnp.float32)],
        flops=4 * 10**9,
        moved=3 * 10**7,
    )


def call(kernel, name, shapes, operands, scratch=(), flops=10**7, moved=4 * 10**6):
    vmem = pl.BlockSpec(memory_space=pltpu.VMEM)
    smem = pl.BlockSpec(memory_space=pltpu.SMEM)
    return pl.pallas_call(
        kernel,
        out_shape=shapes,
        in_specs=[smem if operand.ndim == 1 else vmem for operand in operands],
        out_specs=jax.tree.map(lambda _: vmem, shapes),
        scratch_shapes=scratch,
        compiler_params=pltpu.CompilerParams(vmem_limit_bytes=VMEM_LIMIT),
        cost_estimate=pl.CostEstimate(flops=flops, bytes_accessed=moved, transcendentals=0),
        name=name,
    )(*operands)


def count_kernel(words_ref, spread_ref, kept_ref):
    rows, width = words_ref.shape
    step = 64

    def chunk(at, totals):
        span = pl.ds(pl.multiple_of(at * step, step), step)
        words = words_ref[span, :]
        kept_ref[span, :] = words
        bits = [
            jnp.bitwise_and(jnp.right_shift(words, 2 * place + bit), 1)
            for bit in range(2)
            for place in range(PLACES)
        ]
        return tuple(
            total + jnp.sum(bit.reshape(step // 8, 8, width), axis=0)
            for total, bit in zip(totals, bits)
        )

    zeros = jnp.zeros((8, width), jnp.int32)
    totals = lax.fori_loop(0, rows // step, chunk, (zeros,) * (2 * PLACES))
    shape = (COUNT_ROWS, width)
    sublane = lax.broadcasted_iota(jnp.int32, shape, 0)
    out = jnp.zeros(shape, jnp.float32)
    for index, total in enumerate(totals):
        count = jnp.sum(total.astype(jnp.float32), axis=0, keepdims=True) - rows / 2
        out = jnp.where(sublane == index, jnp.broadcast_to(count, shape), out)
    out = out.astype(jnp.bfloat16)
    for index in range(spread_ref.shape[0]):
        spread_ref[index] = out


def standardize_kernel(counts_ref, words_ref, weight_ref, variant_ref, matrix_ref):
    rows, width = words_ref.shape
    rows_all = rows * counts_ref.shape[0]
    counts = counts_ref[0].astype(jnp.float32)
    for index in range(1, counts_ref.shape[0]):
        counts = counts + counts_ref[index].astype(jnp.float32)
    counts = counts + rows_all / 2
    ones, twos = counts[:PLACES], counts[PLACES : 2 * PLACES]
    mean = (ones + 2 * twos) / rows_all
    scale = lax.rsqrt((ones + 4 * twos) / rows_all - mean * mean + EPSILON) * variant_ref[...]
    step = 64

    def chunk(at, carry):
        span = pl.ds(pl.multiple_of(at * step, step), step)
        words = words_ref[span, :]
        weight = jnp.broadcast_to(weight_ref[span, :], (step, width))
        for place in range(PLACES):
            across = slice(place * width, (place + 1) * width)
            dosage = jnp.bitwise_and(jnp.right_shift(words, 2 * place), 3).astype(jnp.float32)
            value = (dosage - mean[place : place + 1]) * scale[place : place + 1] * weight
            matrix_ref[span, across] = value.astype(jnp.bfloat16)
        return carry

    lax.fori_loop(0, rows // step, chunk, 0)


def sum_spread_kernel(*refs):
    blocks_ref, spread_ref = refs[0], refs[-1]
    total = blocks_ref[0].astype(jnp.float32)
    for index in range(1, blocks_ref.shape[0]):
        total = total + blocks_ref[index].astype(jnp.float32)
    total = total.astype(spread_ref.dtype)
    for index in range(spread_ref.shape[0]):
        spread_ref[index, : total.shape[0]] = total
    if len(refs) == 3:
        tail = refs[1][...]
        for index in range(spread_ref.shape[0]):
            spread_ref[index, total.shape[0] :] = tail


def sum_spread(blocks, *tail):
    count, rows, width = blocks.shape
    rows += sum(part.shape[0] for part in tail)
    shape = jax.ShapeDtypeStruct((count, rows, width), blocks.dtype)
    return call(sum_spread_kernel, "sum_spread", shape, (blocks, *tail))


def product_kernel(core_ref, gathered_ref, product_ref, spread_ref, packed):
    count = gathered_ref.shape[0]
    own = product_ref.shape[0] // count
    for index in range(count):
        product_ref[index * own : (index + 1) * own] = gathered_ref[index, :own]
    product = product_ref[...]
    gram = lax.dot_general(
        product, product, CONTRACT_ROWS, precision=HIGHEST, preferred_element_type=jnp.float32
    )
    packed[...] = pack(gram)
    half = packed.shape[0] // 2
    share = packed[pl.ds(pl.multiple_of(core_ref[0] * half, 8), half), :]
    for index in range(spread_ref.shape[0]):
        spread_ref[index] = share


def apply_factor(panel, inverse):
    return lax.dot_general(panel, inverse, (((1,), (1,)), ((), ())), precision=HIGHEST)


def congruent(gram, factor):
    return apply_factor(jnp.dot(factor, gram, precision=HIGHEST), factor)


def local_gram(panel):
    return lax.dot_general(panel, panel, CONTRACT_ROWS, precision=HIGHEST)


def per_device(dosage_words, sample_weight, variant_weight, omega):
    rows_local, width = dosage_words.shape
    rows_all = rows_local * lax.axis_size("row")
    cols_all = PLACES * width * lax.axis_size("col")
    n_row, n_col = lax.axis_size("row"), lax.axis_size("col")
    counts, words = call(
        count_kernel,
        "count",
        (
            jax.ShapeDtypeStruct((n_row, COUNT_ROWS, width), jnp.bfloat16),
            jax.ShapeDtypeStruct((rows_local, width), jnp.int32),
        ),
        (dosage_words,),
    )
    matrix = call(
        standardize_kernel,
        "standardize",
        jax.ShapeDtypeStruct((rows_local, PLACES * width), jnp.bfloat16),
        (
            exchange(counts, "row"),
            words,
            sample_weight[:, None],
            variant_weight.reshape(PLACES, width),
        ),
    )
    col = lax.axis_index("col")
    own, part = rows_local // n_col, RANK // n_col
    chunk = PLACES * width // n_row

    sketch_part = jnp.dot(matrix, omega, preferred_element_type=jnp.float32)
    arrived = exchange(sketch_part.reshape(n_col, own, RANK), "col")
    sketch = exchange(sum_spread(arrived), "col").reshape(rows_local, RANK)

    sketch_terms = jnp.concatenate(halves(sketch, 2), axis=1)
    spans = [slice(0, n_row * chunk // 2), slice(n_row * chunk // 2, n_row * chunk)]
    arrived = []
    for span in spans:
        terms = lax.dot_general(
            matrix[:, span], sketch_terms, CONTRACT_ROWS, preferred_element_type=jnp.float32
        )
        back_part = (terms[:, :RANK] + terms[:, RANK:]).astype(jnp.bfloat16)
        arrived.append(exchange(back_part.reshape(n_row, chunk // 2, RANK), "row"))
    gram_share = lax.dynamic_slice_in_dim(local_gram(sketch), col * part, part, 0)
    share_terms = jnp.concatenate(
        halves(gram_share, 3) + [jnp.zeros((part, RANK), jnp.bfloat16)], axis=0
    )
    first_half = exchange(sum_spread(arrived[0]), "row")
    last_half = exchange(sum_spread(arrived[1], share_terms), "row")
    gram_share = jnp.sum(
        last_half[:, chunk // 2 :].astype(jnp.float32).reshape(4 * n_row, part, RANK), axis=0
    )
    back = jnp.concatenate(
        [
            first_half.reshape(n_row * chunk // 2, RANK),
            last_half[:, : chunk // 2].reshape(n_row * chunk // 2, RANK),
        ],
        axis=0,
    )

    product_part = jnp.dot(matrix, back, preferred_element_type=jnp.float32)
    back_gram = lax.dot_general(back, back, CONTRACT_ROWS, preferred_element_type=jnp.float32)
    back_gram = lax.optimization_barrier(back_gram)
    arrived = exchange(
        jnp.concatenate(
            [
                product_part.reshape(n_col, own, RANK),
                back_gram.reshape(n_col, part, RANK),
                jnp.broadcast_to(gram_share[None], (n_col, part, RANK)),
            ],
            axis=1,
        ),
        "col",
    )
    sketch_factor = inverse_factor(arrived[:, own + part :].reshape(RANK, RANK))
    gathered = exchange(sum_spread(arrived), "col")
    gathered, sketch_factor = lax.optimization_barrier((gathered, sketch_factor))
    back_gram = gathered[:, own : own + part].reshape(RANK, RANK)

    core = lax.rem(col, 2)
    product, spread = call(
        product_kernel,
        "product",
        (
            jax.ShapeDtypeStruct((rows_local, RANK), jnp.float32),
            jax.ShapeDtypeStruct((n_row, PACKED_ROWS // 2, RANK), jnp.float32),
        ),
        (core.reshape(1), gathered),
        scratch=[pltpu.VMEM((PACKED_ROWS, RANK), jnp.float32)],
    )
    gathered = exchange(spread, "row")
    back_factor = inverse_factor(congruent(back_gram, sketch_factor))
    factor = jnp.dot(back_factor, sketch_factor, precision=HIGHEST)
    right_full = apply_factor(back.astype(jnp.float32), factor)
    product = apply_factor(product, factor)
    gathered, product = lax.optimization_barrier((gathered, product))
    packed = jnp.sum(gathered, axis=0)
    other = lax.ppermute(packed, "col", [(index, index ^ 1) for index in range(n_col)])
    packed = jnp.where(
        core == 0,
        jnp.concatenate([packed, other], axis=0),
        jnp.concatenate([other, packed], axis=0),
    )
    gram = congruent(symmetric(unpack_upper(packed)), factor)
    second = apply_factor(product, inverse_factor(gram))
    second_own = lax.dynamic_slice_in_dim(second, col * own, own, 0)

    projection_part = lax.dot_general(
        second.astype(jnp.bfloat16), matrix, CONTRACT_ROWS, preferred_element_type=jnp.float32
    ).astype(jnp.bfloat16)
    arrived = exchange(projection_part.reshape(n_row, RANK // n_row, -1), "row")
    projection = jnp.sum(arrived.astype(jnp.float32), axis=0).T
    return (second_own * math.sqrt(rows_all), right_full * math.sqrt(cols_all), projection)


def solution(mesh):
    in_specs = (P("row", "col"), P("row"), P("col"), P("col", None))
    out_specs = (P(("row", "col"), None), P("col", None), P("col", "row"))
    return jax.shard_map(
        per_device, mesh=mesh, in_specs=in_specs, out_specs=out_specs, check_vma=False
    )
```

```python
import math

import jax
import jax.numpy as jnp
from jax import lax
from jax.experimental import pallas as pl
from jax.experimental.pallas import tpu as pltpu
from jax.sharding import PartitionSpec as P

EPSILON = 1e-05
PLACES = 6
RANK = 128
COUNT_ROWS = 16
NEAR = 8
CONTRACT_ROWS = (((0,), (0,)), ((), ()))
HIGHEST = lax.Precision.HIGHEST
VMEM_LIMIT = 32 * 1024 * 1024
BLOCK = 16
SUBLANES = 8


def exchange(blocks, axis, groups=None):
    return lax.all_to_all(
        blocks, axis, split_axis=0, concat_axis=0, axis_index_groups=groups, tiled=True
    )


def halves(values, count):
    terms = []
    for index in range(count):
        term = lax.reduce_precision(values, exponent_bits=8, mantissa_bits=7)
        values = values - term
        terms.append(term.astype(jnp.bfloat16))
    return terms


def inverse_factor_kernel(gram_ref, inverse_ref, work):
    size = gram_ref.shape[0]
    whole, tile = (BLOCK, size), (SUBLANES, size)
    work[...] = gram_ref[...]
    lane = lax.broadcasted_iota(jnp.int32, whole, 1)
    row_at = lax.broadcasted_iota(jnp.int32, whole, 0)
    sublane = lax.broadcasted_iota(jnp.int32, tile, 0)
    all_lanes = lax.broadcasted_iota(jnp.int32, (size, size), 1)

    def spread(rows):
        tiles = []
        for first in range(0, BLOCK, SUBLANES):
            out = rows[first]
            for index in range(1, SUBLANES):
                out = jnp.where(sublane == index, rows[first + index], out)
            tiles.append(out)
        return jnp.concatenate(tiles, axis=0)

    def step(at, carry):
        base = pl.multiple_of(at * BLOCK, BLOCK)
        rows = work[pl.ds(base, BLOCK), :]
        turned = pltpu.roll(rows, lax.rem(size - base, size), 1)
        columns = [jnp.broadcast_to(turned[:, j : j + 1], whole) for j in range(BLOCK)]
        entry = {
            (i, j): jnp.broadcast_to(columns[i][j : j + 1, :], tile)
            for j in range(BLOCK)
            for i in range(j, BLOCK)
        }
        within = jnp.logical_and(lane >= base, lane < base + BLOCK)
        start = jnp.where(within, (lane - base == row_at).astype(jnp.float32), rows)
        done, pivots, reciprocals = [], [], []
        for j in range(BLOCK):
            row = jnp.broadcast_to(start[j : j + 1, :], tile)
            for k in range(j):
                row = row - entry[j, k] * done[k]
            done.append(row)
            pivots.append(entry[j, j])
            reciprocal = 1.0 / entry[j, j]
            reciprocals.append(reciprocal)
            factors = {i: entry[i, j] * reciprocal for i in range(j + 1, BLOCK)}
            for i in range(j + 1, BLOCK):
                for k in range(j + 1, i + 1):
                    entry[i, k] = entry[i, k] - factors[i] * entry[k, j]
            for i in range(j + 1, BLOCK):
                entry[i, j] = factors[i]
        block = spread(done)
        inverse_ref[pl.ds(base, BLOCK), :] = jnp.where(
            lane < base + BLOCK, block, 0.0
        ) * lax.rsqrt(spread(pivots))
        factor = jnp.where(lane >= base + BLOCK, block * spread(reciprocals), 0.0)
        update = lax.dot_general(
            factor, block, CONTRACT_ROWS, precision=HIGHEST, preferred_element_type=jnp.float32
        )
        inside = jnp.logical_and(all_lanes >= base, all_lanes < base + BLOCK)
        work[...] = jnp.where(inside, 0.0, work[...]) - update
        return carry

    lax.fori_loop(0, size // BLOCK, step, 0)


def inverse_factor(gram_sum):
    return call(
        inverse_factor_kernel,
        "inverse_factor",
        jax.ShapeDtypeStruct(gram_sum.shape, jnp.float32),
        (gram_sum,),
        scratch=[pltpu.VMEM(gram_sum.shape, jnp.float32)],
        flops=4 * 10**9,
        moved=3 * 10**7,
    )


def call(kernel, name, shapes, operands, scratch=(), flops=10**7, moved=4 * 10**6):
    vmem = pl.BlockSpec(memory_space=pltpu.VMEM)
    smem = pl.BlockSpec(memory_space=pltpu.SMEM)
    return pl.pallas_call(
        kernel,
        out_shape=shapes,
        in_specs=[smem if operand.ndim == 1 else vmem for operand in operands],
        out_specs=jax.tree.map(lambda _: vmem, shapes),
        scratch_shapes=scratch,
        compiler_params=pltpu.CompilerParams(vmem_limit_bytes=VMEM_LIMIT),
        cost_estimate=pl.CostEstimate(flops=flops, bytes_accessed=moved, transcendentals=0),
        name=name,
    )(*operands)


def count_kernel(words_ref, spread_ref, kept_ref):
    rows, width = words_ref.shape
    step = 64

    def chunk(at, totals):
        span = pl.ds(pl.multiple_of(at * step, step), step)
        words = words_ref[span, :]
        kept_ref[span, :] = words
        bits = [
            jnp.bitwise_and(jnp.right_shift(words, 2 * place + bit), 1)
            for bit in range(2)
            for place in range(PLACES)
        ]
        return tuple(
            total + jnp.sum(bit.reshape(step // 8, 8, width), axis=0)
            for total, bit in zip(totals, bits)
        )

    zeros = jnp.zeros((8, width), jnp.int32)
    totals = lax.fori_loop(0, rows // step, chunk, (zeros,) * (2 * PLACES))
    shape = (COUNT_ROWS, width)
    sublane = lax.broadcasted_iota(jnp.int32, shape, 0)
    out = jnp.zeros(shape, jnp.float32)
    for index, total in enumerate(totals):
        count = jnp.sum(total.astype(jnp.float32), axis=0, keepdims=True) - rows / 2
        out = jnp.where(sublane == index, jnp.broadcast_to(count, shape), out)
    out = out.astype(jnp.bfloat16)
    for index in range(spread_ref.shape[0]):
        spread_ref[index] = out


def standardize_kernel(counts_ref, words_ref, weight_ref, variant_ref, matrix_ref):
    rows, width = words_ref.shape
    rows_all = rows * counts_ref.shape[0]
    counts = counts_ref[0].astype(jnp.float32)
    for index in range(1, counts_ref.shape[0]):
        counts = counts + counts_ref[index].astype(jnp.float32)
    counts = counts + rows_all / 2
    ones, twos = counts[:PLACES], counts[PLACES : 2 * PLACES]
    mean = (ones + 2 * twos) / rows_all
    scale = lax.rsqrt((ones + 4 * twos) / rows_all - mean * mean + EPSILON) * variant_ref[...]
    step = 64

    def chunk(at, carry):
        span = pl.ds(pl.multiple_of(at * step, step), step)
        words = words_ref[span, :]
        weight = jnp.broadcast_to(weight_ref[span, :], (step, width))
        for place in range(PLACES):
            across = slice(place * width, (place + 1) * width)
            dosage = jnp.bitwise_and(jnp.right_shift(words, 2 * place), 3).astype(jnp.float32)
            value = (dosage - mean[place : place + 1]) * scale[place : place + 1] * weight
            matrix_ref[span, across] = value.astype(jnp.bfloat16)
        return carry

    lax.fori_loop(0, rows // step, chunk, 0)


def sum_spread_kernel(*refs):
    blocks_ref, spread_ref = refs[0], refs[-1]
    total = blocks_ref[0].astype(jnp.float32)
    for index in range(1, blocks_ref.shape[0]):
        total = total + blocks_ref[index].astype(jnp.float32)
    total = total.astype(spread_ref.dtype)
    for index in range(spread_ref.shape[0]):
        spread_ref[index, : total.shape[0]] = total
    if len(refs) == 3:
        tail = refs[1][...]
        for index in range(spread_ref.shape[0]):
            spread_ref[index, total.shape[0] :] = tail


def sum_spread(blocks, *tail, count=None):
    rows, width = blocks.shape[1:]
    count = count or blocks.shape[0]
    rows += sum(part.shape[0] for part in tail)
    shape = jax.ShapeDtypeStruct((count, rows, width), blocks.dtype)
    return call(sum_spread_kernel, "sum_spread", shape, (blocks, *tail))


def product_kernel(place_ref, gathered_ref, product_ref, spread_ref, gram):
    count = gathered_ref.shape[0]
    own = product_ref.shape[0] // count
    for index in range(count):
        product_ref[index * own : (index + 1) * own] = gathered_ref[index, :own]
    product = product_ref[...]
    gram[...] = lax.dot_general(
        product, product, CONTRACT_ROWS, precision=HIGHEST, preferred_element_type=jnp.float32
    )
    share = gram.shape[0] // NEAR
    rows = gram[pl.ds(pl.multiple_of(place_ref[0] * share, share), share), :]
    for index in range(spread_ref.shape[0]):
        spread_ref[index] = rows


def apply_factor(panel, inverse):
    return lax.dot_general(panel, inverse, (((1,), (1,)), ((), ())), precision=HIGHEST)


def congruent(gram, factor):
    return apply_factor(jnp.dot(factor, gram, precision=HIGHEST), factor)


def local_gram(panel):
    return lax.dot_general(panel, panel, CONTRACT_ROWS, precision=HIGHEST)


def per_device(dosage_words, sample_weight, variant_weight, omega):
    rows_local, width = dosage_words.shape
    rows_all = rows_local * lax.axis_size("row")
    cols_all = PLACES * width * lax.axis_size("col")
    n_row, n_col = lax.axis_size("row"), lax.axis_size("col")
    counts, words = call(
        count_kernel,
        "count",
        (
            jax.ShapeDtypeStruct((n_row, COUNT_ROWS, width), jnp.bfloat16),
            jax.ShapeDtypeStruct((rows_local, width), jnp.int32),
        ),
        (dosage_words,),
    )
    matrix = call(
        standardize_kernel,
        "standardize",
        jax.ShapeDtypeStruct((rows_local, PLACES * width), jnp.bfloat16),
        (
            exchange(counts, "row"),
            words,
            sample_weight[:, None],
            variant_weight.reshape(PLACES, width),
        ),
    )
    col = lax.axis_index("col")
    own, part = rows_local // n_col, RANK // n_col
    chunk = PLACES * width // n_row

    sketch_part = jnp.dot(matrix, omega, preferred_element_type=jnp.float32)
    arrived = exchange(sketch_part.reshape(n_col, own, RANK), "col")
    sketch = exchange(sum_spread(arrived), "col").reshape(rows_local, RANK)

    sketch_terms = jnp.concatenate(halves(sketch, 2), axis=1)
    back_terms = lax.dot_general(
        matrix, sketch_terms, CONTRACT_ROWS, preferred_element_type=jnp.float32
    )
    back_part = (back_terms[:, :RANK] + back_terms[:, RANK:]).astype(jnp.bfloat16)
    arrived = exchange(back_part.reshape(n_row, chunk, RANK), "row")
    gram_share = lax.dynamic_slice_in_dim(local_gram(sketch), col * part, part, 0)
    share_terms = jnp.concatenate(
        halves(gram_share, 3) + [jnp.zeros((part, RANK), jnp.bfloat16)], axis=0
    )
    arrived, share_terms = lax.optimization_barrier((arrived, share_terms))
    gathered = exchange(sum_spread(arrived, share_terms), "row")
    back = gathered[:, :chunk].reshape(n_row * chunk, RANK)
    gram_share = jnp.sum(
        gathered[:, chunk:].astype(jnp.float32).reshape(4 * n_row, part, RANK), axis=0
    )

    product_part = jnp.dot(matrix, back, preferred_element_type=jnp.float32)
    back_gram = lax.dot_general(back, back, CONTRACT_ROWS, preferred_element_type=jnp.float32)
    back_gram = lax.optimization_barrier(back_gram)
    arrived = exchange(
        jnp.concatenate(
            [
                product_part.reshape(n_col, own, RANK),
                back_gram.reshape(n_col, part, RANK),
                jnp.broadcast_to(gram_share[None], (n_col, part, RANK)),
            ],
            axis=1,
        ),
        "col",
    )
    sketch_factor = inverse_factor(arrived[:, own + part :].reshape(RANK, RANK))
    gathered = exchange(sum_spread(arrived), "col")
    gathered, sketch_factor = lax.optimization_barrier((gathered, sketch_factor))
    back_gram = gathered[:, own : own + part].reshape(RANK, RANK)

    place = lax.rem(col, NEAR)
    product, spread = call(
        product_kernel,
        "product",
        (
            jax.ShapeDtypeStruct((rows_local, RANK), jnp.float32),
            jax.ShapeDtypeStruct((n_row, RANK // NEAR, RANK), jnp.float32),
        ),
        (place.reshape(1), gathered),
        scratch=[pltpu.VMEM((RANK, RANK), jnp.float32)],
    )
    gathered = exchange(spread, "row")
    back_factor = inverse_factor(congruent(back_gram, sketch_factor))
    factor = jnp.dot(back_factor, sketch_factor, precision=HIGHEST)
    right_full = apply_factor(back.astype(jnp.float32), factor)
    product = apply_factor(product, factor)
    gathered, product = lax.optimization_barrier((gathered, product))
    near = [list(range(first, first + NEAR)) for first in range(0, n_col, NEAR)]
    gram = exchange(sum_spread(gathered, count=NEAR), "col", near).reshape(RANK, RANK)
    gram = congruent(gram, factor)
    second = apply_factor(product, inverse_factor(gram))
    second_own = lax.dynamic_slice_in_dim(second, col * own, own, 0)

    projection_part = lax.dot_general(
        second.astype(jnp.bfloat16), matrix, CONTRACT_ROWS, preferred_element_type=jnp.float32
    ).astype(jnp.bfloat16)
    arrived = exchange(projection_part.reshape(n_row, RANK // n_row, -1), "row")
    projection = jnp.sum(arrived.astype(jnp.float32), axis=0).T
    return (second_own * math.sqrt(rows_all), right_full * math.sqrt(cols_all), projection)


def solution(mesh):
    in_specs = (P("row", "col"), P("row"), P("col"), P("col", None))
    out_specs = (P(("row", "col"), None), P("col", None), P("col", "row"))
    return jax.shard_map(
        per_device, mesh=mesh, in_specs=in_specs, out_specs=out_specs, check_vma=False
    )
```

```python
import math

import jax
import jax.numpy as jnp
from jax import lax
from jax.experimental import pallas as pl
from jax.experimental.pallas import tpu as pltpu
from jax.sharding import PartitionSpec as P

EPSILON = 1e-05
PLACES = 6
RANK = 128
COUNT_ROWS = 16
NEAR = 8
CONTRACT_ROWS = (((0,), (0,)), ((), ()))
HIGHEST = lax.Precision.HIGHEST
VMEM_LIMIT = 32 * 1024 * 1024
BLOCK = 16
SUBLANES = 8
WORD_PIECES = 4


def exchange(blocks, axis, groups=None):
    return lax.all_to_all(
        blocks, axis, split_axis=0, concat_axis=0, axis_index_groups=groups, tiled=True
    )


def halves(values, count):
    terms = []
    for index in range(count):
        term = lax.reduce_precision(values, exponent_bits=8, mantissa_bits=7)
        values = values - term
        terms.append(term.astype(jnp.bfloat16))
    return terms


def inverted(values):
    guess = pl.reciprocal(values, approx=True)
    for _ in range(2):
        guess = guess * (2.0 - values * guess)
    return guess


def inverse_factor_kernel(*refs):
    gram_ref, inverse_ref, work = refs[0], refs[-2], refs[-1]
    size = gram_ref.shape[0]
    whole, tile = (BLOCK, size), (SUBLANES, size)
    work[...] = congruent(gram_ref[...], refs[1][...]) if len(refs) == 4 else gram_ref[...]
    lane = lax.broadcasted_iota(jnp.int32, whole, 1)
    row_at = lax.broadcasted_iota(jnp.int32, whole, 0)
    sublane = lax.broadcasted_iota(jnp.int32, tile, 0)
    all_lanes = lax.broadcasted_iota(jnp.int32, (size, size), 1)

    def spread(rows):
        tiles = []
        for first in range(0, BLOCK, SUBLANES):
            out = rows[first]
            for index in range(1, SUBLANES):
                out = jnp.where(sublane == index, rows[first + index], out)
            tiles.append(out)
        return jnp.concatenate(tiles, axis=0)

    def step(at, carry):
        base = pl.multiple_of(at * BLOCK, BLOCK)
        rows = work[pl.ds(base, BLOCK), :]
        turned = pltpu.roll(rows, lax.rem(size - base, size), 1)
        columns = [jnp.broadcast_to(turned[:, j : j + 1], whole) for j in range(BLOCK)]
        entry = {
            (i, j): jnp.broadcast_to(columns[i][j : j + 1, :], tile)
            for j in range(BLOCK)
            for i in range(j, BLOCK)
        }
        within = jnp.logical_and(lane >= base, lane < base + BLOCK)
        start = jnp.where(within, (lane - base == row_at).astype(jnp.float32), rows)
        done, pivots, reciprocals = [], [], []
        for j in range(BLOCK):
            row = jnp.broadcast_to(start[j : j + 1, :], tile)
            for k in range(j):
                row = row - entry[j, k] * done[k]
            done.append(row)
            pivots.append(entry[j, j])
            reciprocal = inverted(entry[j, j])
            reciprocals.append(reciprocal)
            factors = {i: entry[i, j] * reciprocal for i in range(j + 1, BLOCK)}
            for i in range(j + 1, BLOCK):
                for k in range(j + 1, i + 1):
                    if k == j + 1:
                        change = (entry[i, j] * entry[k, j]) * reciprocal
                    else:
                        change = factors[i] * entry[k, j]
                    entry[i, k] = entry[i, k] - change
            for i in range(j + 1, BLOCK):
                entry[i, j] = factors[i]
        block = spread(done)
        inverse_ref[pl.ds(base, BLOCK), :] = jnp.where(
            lane < base + BLOCK, block, 0.0
        ) * lax.rsqrt(spread(pivots))
        factor = jnp.where(lane >= base + BLOCK, block * spread(reciprocals), 0.0)
        update = lax.dot_general(
            factor, block, CONTRACT_ROWS, precision=HIGHEST, preferred_element_type=jnp.float32
        )
        inside = jnp.logical_and(all_lanes >= base, all_lanes < base + BLOCK)
        work[...] = jnp.where(inside, 0.0, work[...]) - update
        return carry

    lax.fori_loop(0, size // BLOCK, step, 0)


def inverse_factor(gram_sum, *factor):
    return call(
        inverse_factor_kernel,
        "inverse_factor",
        jax.ShapeDtypeStruct(gram_sum.shape, jnp.float32),
        (gram_sum, *factor),
        scratch=[pltpu.VMEM(gram_sum.shape, jnp.float32)],
        flops=4 * 10**9,
        moved=3 * 10**7,
    )


def call(
    kernel, name, shapes, operands, scratch=(), specs=None, flops=10**7, moved=4 * 10**6
):
    vmem = pl.BlockSpec(memory_space=pltpu.VMEM)
    smem = pl.BlockSpec(memory_space=pltpu.SMEM)
    return pl.pallas_call(
        kernel,
        out_shape=shapes,
        in_specs=specs or [smem if operand.ndim == 1 else vmem for operand in operands],
        out_specs=jax.tree.map(lambda _: vmem, shapes),
        scratch_shapes=scratch,
        compiler_params=pltpu.CompilerParams(vmem_limit_bytes=VMEM_LIMIT),
        cost_estimate=pl.CostEstimate(flops=flops, bytes_accessed=moved, transcendentals=0),
        name=name,
    )(*operands)


def count_kernel(words_ref, spread_ref, kept_ref, arrived):
    rows, width = words_ref.shape
    step = 64
    pieces = arrived.shape[0]
    copies = []
    for index in range(pieces):
        span = pl.ds(index * (rows // pieces), rows // pieces)
        copies.append(
            pltpu.make_async_copy(words_ref.at[span, :], kept_ref.at[span, :], arrived.at[index])
        )
        copies[-1].start()

    def chunk(at, totals):
        words = kept_ref[pl.ds(pl.multiple_of(at * step, step), step), :]
        bits = [
            jnp.bitwise_and(jnp.right_shift(words, 2 * place + bit), 1)
            for bit in range(2)
            for place in range(PLACES)
        ]
        return tuple(
            total + jnp.sum(bit.reshape(step // 8, 8, width), axis=0)
            for total, bit in zip(totals, bits)
        )

    zeros = jnp.zeros((8, width), jnp.int32)
    totals = (zeros,) * (2 * PLACES)
    steps = rows // step // pieces
    for index, copy in enumerate(copies):
        copy.wait()
        totals = lax.fori_loop(index * steps, (index + 1) * steps, chunk, totals)
    shape = (COUNT_ROWS, width)
    sublane = lax.broadcasted_iota(jnp.int32, shape, 0)
    out = jnp.zeros(shape, jnp.float32)
    for index, total in enumerate(totals):
        count = jnp.sum(total.astype(jnp.float32), axis=0, keepdims=True) - rows / 2
        out = jnp.where(sublane == index, jnp.broadcast_to(count, shape), out)
    out = out.astype(jnp.bfloat16)
    for index in range(spread_ref.shape[0]):
        spread_ref[index] = out


def standardize_kernel(counts_ref, words_ref, weight_ref, variant_ref, matrix_ref):
    rows, width = words_ref.shape
    rows_all = rows * counts_ref.shape[0]
    counts = counts_ref[0].astype(jnp.float32)
    for index in range(1, counts_ref.shape[0]):
        counts = counts + counts_ref[index].astype(jnp.float32)
    counts = counts + rows_all / 2
    ones, twos = counts[:PLACES], counts[PLACES : 2 * PLACES]
    mean = (ones + 2 * twos) / rows_all
    scale = lax.rsqrt((ones + 4 * twos) / rows_all - mean * mean + EPSILON) * variant_ref[...]
    step = 64

    def chunk(at, carry):
        span = pl.ds(pl.multiple_of(at * step, step), step)
        words = words_ref[span, :]
        weight = jnp.broadcast_to(weight_ref[span, :], (step, width))
        for place in range(PLACES):
            across = slice(place * width, (place + 1) * width)
            dosage = jnp.bitwise_and(jnp.right_shift(words, 2 * place), 3).astype(jnp.float32)
            value = (dosage - mean[place : place + 1]) * scale[place : place + 1] * weight
            matrix_ref[span, across] = value.astype(jnp.bfloat16)
        return carry

    lax.fori_loop(0, rows // step, chunk, 0)


def sum_spread_kernel(blocks_ref, spread_ref):
    total = blocks_ref[0]
    for index in range(1, blocks_ref.shape[0]):
        total = total + blocks_ref[index]
    for index in range(spread_ref.shape[0]):
        spread_ref[index] = total


def sum_spread(blocks, count=None):
    rows, width = blocks.shape[1:]
    shape = jax.ShapeDtypeStruct((count or blocks.shape[0], rows, width), jnp.float32)
    return call(sum_spread_kernel, "sum_spread", shape, (blocks,))


def product_kernel(place_ref, gathered_ref, product_ref, spread_ref, gram):
    count = gathered_ref.shape[0]
    own = product_ref.shape[0] // count
    for index in range(count):
        product_ref[index * own : (index + 1) * own] = gathered_ref[index, :own]
    product = product_ref[...]
    gram[...] = lax.dot_general(
        product, product, CONTRACT_ROWS, precision=HIGHEST, preferred_element_type=jnp.float32
    )
    share = gram.shape[0] // NEAR
    rows = gram[pl.ds(pl.multiple_of(place_ref[0] * share, share), share), :]
    for index in range(spread_ref.shape[0]):
        spread_ref[index] = rows


def apply_factor(panel, inverse):
    return lax.dot_general(
        panel, inverse, (((1,), (1,)), ((), ())), precision=HIGHEST, preferred_element_type=jnp.float32
    )


def congruent(gram, factor):
    half = lax.dot_general(
        factor, gram, (((1,), (0,)), ((), ())), precision=HIGHEST, preferred_element_type=jnp.float32
    )
    return apply_factor(half, factor)


def local_gram(panel):
    return lax.dot_general(panel, panel, CONTRACT_ROWS, precision=HIGHEST)


def per_device(dosage_words, sample_weight, variant_weight, omega):
    rows_local, width = dosage_words.shape
    rows_all = rows_local * lax.axis_size("row")
    cols_all = PLACES * width * lax.axis_size("col")
    n_row, n_col = lax.axis_size("row"), lax.axis_size("col")
    counts, words = call(
        count_kernel,
        "count",
        (
            jax.ShapeDtypeStruct((n_row, COUNT_ROWS, width), jnp.bfloat16),
            jax.ShapeDtypeStruct((rows_local, width), jnp.int32),
        ),
        (dosage_words,),
        scratch=[pltpu.SemaphoreType.DMA((WORD_PIECES,))],
        specs=[pl.BlockSpec(memory_space=pltpu.HBM)],
    )
    matrix = call(
        standardize_kernel,
        "standardize",
        jax.ShapeDtypeStruct((rows_local, PLACES * width), jnp.bfloat16),
        (
            exchange(counts, "row"),
            words,
            sample_weight[:, None],
            variant_weight.reshape(PLACES, width),
        ),
    )
    col = lax.axis_index("col")
    own, part = rows_local // n_col, RANK // n_col
    chunk = PLACES * width // n_row

    sketch_part = jnp.dot(matrix, omega, preferred_element_type=jnp.float32)
    arrived = exchange(sketch_part.reshape(n_col, own, RANK), "col")
    sketch = exchange(sum_spread(arrived), "col").reshape(rows_local, RANK)

    back_part = lax.dot_general(
        matrix, sketch.astype(jnp.bfloat16), CONTRACT_ROWS, preferred_element_type=jnp.float32
    ).astype(jnp.bfloat16)
    arrived = exchange(back_part.reshape(n_row, chunk, RANK), "row")
    gram_share = lax.dynamic_slice_in_dim(local_gram(sketch), col * part, part, 0)
    share_terms = jnp.concatenate(
        halves(gram_share, 3) + [jnp.zeros((part, RANK), jnp.bfloat16)], axis=0
    )
    arrived, share_terms = lax.optimization_barrier((arrived, share_terms))
    back_own = jnp.sum(arrived.astype(jnp.float32), axis=0).astype(jnp.bfloat16)
    back_own = jnp.concatenate([back_own, share_terms], axis=0)
    gathered = lax.all_gather(back_own, "row", axis=0, tiled=True)
    gathered = gathered.reshape(n_row, chunk + 4 * part, RANK)
    back = gathered[:, :chunk].reshape(n_row * chunk, RANK)
    gram_share = jnp.sum(
        gathered[:, chunk:].astype(jnp.float32).reshape(4 * n_row, part, RANK), axis=0
    )

    product_part = jnp.dot(matrix, back, preferred_element_type=jnp.float32)
    back_gram = lax.dot_general(back, back, CONTRACT_ROWS, preferred_element_type=jnp.float32)
    back_gram = lax.optimization_barrier(back_gram)
    arrived = exchange(
        jnp.concatenate(
            [
                product_part.reshape(n_col, own, RANK),
                back_gram.reshape(n_col, part, RANK),
                jnp.broadcast_to(gram_share[None], (n_col, part, RANK)),
            ],
            axis=1,
        ),
        "col",
    )
    sketch_factor = inverse_factor(arrived[:, own + part :].reshape(RANK, RANK))
    gathered = exchange(sum_spread(arrived), "col")
    gathered, sketch_factor = lax.optimization_barrier((gathered, sketch_factor))
    back_gram = gathered[:, own : own + part].reshape(RANK, RANK)

    place = lax.rem(col, NEAR)
    product, spread = call(
        product_kernel,
        "product",
        (
            jax.ShapeDtypeStruct((rows_local, RANK), jnp.float32),
            jax.ShapeDtypeStruct((n_row, RANK // NEAR, RANK), jnp.float32),
        ),
        (place.reshape(1), gathered),
        scratch=[pltpu.VMEM((RANK, RANK), jnp.float32)],
    )
    gathered = exchange(spread, "row")
    back_factor = inverse_factor(back_gram, sketch_factor)
    factor = jnp.dot(back_factor, sketch_factor, precision=HIGHEST)
    right_full = apply_factor(back.astype(jnp.float32), factor)
    product = apply_factor(product, factor)
    gathered, product = lax.optimization_barrier((gathered, product))
    near = [list(range(first, first + NEAR)) for first in range(0, n_col, NEAR)]
    gram = exchange(sum_spread(gathered, count=NEAR), "col", near).reshape(RANK, RANK)
    second = apply_factor(product, inverse_factor(gram, factor))
    second_own = lax.dynamic_slice_in_dim(second, col * own, own, 0)

    projection_part = lax.dot_general(
        second.astype(jnp.bfloat16), matrix, CONTRACT_ROWS, preferred_element_type=jnp.float32
    ).astype(jnp.bfloat16)
    arrived = exchange(projection_part.reshape(n_row, RANK // n_row, -1), "row")
    projection = jnp.sum(arrived.astype(jnp.float32), axis=0).T
    return (second_own * math.sqrt(rows_all), right_full * math.sqrt(cols_all), projection)


def solution(mesh):
    in_specs = (P("row", "col"), P("row"), P("col"), P("col", None))
    out_specs = (P(("row", "col"), None), P("col", None), P("col", "row"))
    return jax.shard_map(
        per_device, mesh=mesh, in_specs=in_specs, out_specs=out_specs, check_vma=False
    )
```

```python
import functools
import math

import jax
import jax.numpy as jnp
from jax import lax
from jax.experimental import pallas as pl
from jax.experimental.pallas import tpu as pltpu
from jax.sharding import PartitionSpec as P

EPSILON = 1e-05
PLACES = 6
RANK = 128
COUNT_ROWS = 16
NEAR = 8
CONTRACT_ROWS = (((0,), (0,)), ((), ()))
HIGHEST = lax.Precision.HIGHEST
VMEM_LIMIT = 32 * 1024 * 1024
BLOCK = 16
SUBLANES, LANES = 8, 128


def exchange(blocks, axis, groups=None):
    return lax.all_to_all(
        blocks, axis, split_axis=0, concat_axis=0, axis_index_groups=groups, tiled=True
    )


def halves(values, count):
    terms = []
    for index in range(count):
        term = lax.reduce_precision(values, exponent_bits=8, mantissa_bits=7)
        values = values - term
        terms.append(term.astype(jnp.bfloat16))
    return terms


def eliminate(inverse_ref, work):
    size = work.shape[0]
    whole, tile = (BLOCK, size), (SUBLANES, size)
    lane = lax.broadcasted_iota(jnp.int32, whole, 1)
    row_at = lax.broadcasted_iota(jnp.int32, whole, 0)
    sublane = lax.broadcasted_iota(jnp.int32, tile, 0)
    all_lanes = lax.broadcasted_iota(jnp.int32, (size, size), 1)

    def spread(rows):
        tiles = []
        for first in range(0, BLOCK, SUBLANES):
            out = rows[first]
            for index in range(1, SUBLANES):
                out = jnp.where(sublane == index, rows[first + index], out)
            tiles.append(out)
        return jnp.concatenate(tiles, axis=0)

    def step(at, carry):
        base = pl.multiple_of(at * BLOCK, BLOCK)
        rows = work[pl.ds(base, BLOCK), :]
        turned = pltpu.roll(rows, lax.rem(size - base, size), 1)
        columns = [jnp.broadcast_to(turned[:, j : j + 1], whole) for j in range(BLOCK)]
        entry = {
            (i, j): jnp.broadcast_to(columns[i][j : j + 1, :], tile)
            for j in range(BLOCK)
            for i in range(j, BLOCK)
        }
        within = jnp.logical_and(lane >= base, lane < base + BLOCK)
        start = jnp.where(within, (lane - base == row_at).astype(jnp.float32), rows)
        done, pivots, reciprocals = [], [], []
        for j in range(BLOCK):
            row = jnp.broadcast_to(start[j : j + 1, :], tile)
            for k in range(j):
                row = row - entry[j, k] * done[k]
            done.append(row)
            pivots.append(entry[j, j])
            reciprocal = 1.0 / entry[j, j]
            reciprocals.append(reciprocal)
            factors = {i: entry[i, j] * reciprocal for i in range(j + 1, BLOCK)}
            for i in range(j + 1, BLOCK):
                for k in range(j + 1, i + 1):
                    entry[i, k] = entry[i, k] - factors[i] * entry[k, j]
            for i in range(j + 1, BLOCK):
                entry[i, j] = factors[i]
        block = spread(done)
        inverse_ref[pl.ds(base, BLOCK), :] = jnp.where(
            lane < base + BLOCK, block, 0.0
        ) * lax.rsqrt(spread(pivots))
        factor = jnp.where(lane >= base + BLOCK, block * spread(reciprocals), 0.0)
        update = lax.dot_general(
            factor, block, CONTRACT_ROWS, precision=HIGHEST, preferred_element_type=jnp.float32
        )
        inside = jnp.logical_and(all_lanes >= base, all_lanes < base + BLOCK)
        work[...] = jnp.where(inside, 0.0, work[...]) - update
        return carry

    lax.fori_loop(0, size // BLOCK, step, 0)


def inverse_factor_kernel(*refs):
    work = refs[-1]
    work[...] = refs[0][...] if len(refs) == 3 else congruent(refs[0][...], refs[1][...])
    eliminate(refs[-2], work)


def inverse_factor(gram_sum, *factor):
    return call(
        inverse_factor_kernel,
        "inverse_factor",
        jax.ShapeDtypeStruct(gram_sum.shape, jnp.float32),
        (gram_sum, *factor),
        scratch=[pltpu.VMEM(gram_sum.shape, jnp.float32)],
        flops=4 * 10**9,
        moved=3 * 10**7,
    )


def second_kernel(
    root, col_ref, gram_ref, factor_ref, product_ref, own_ref, half_ref, inverse, work
):
    work[...] = congruent(gram_ref[...], factor_ref[...])
    eliminate(inverse, work)
    half_ref[...] = apply_factor(product_ref[...], inverse[...]).astype(jnp.bfloat16)
    own = own_ref.shape[0]
    rows = product_ref[pl.ds(pl.multiple_of(col_ref[0] * own, own), own), :]
    own_ref[...] = apply_factor(rows, inverse[...]) * root


def call(kernel, name, shapes, operands, scratch=(), flops=10**7, moved=4 * 10**6):
    vmem = pl.BlockSpec(memory_space=pltpu.VMEM)
    smem = pl.BlockSpec(memory_space=pltpu.SMEM)
    return pl.pallas_call(
        kernel,
        out_shape=shapes,
        in_specs=[smem if operand.ndim == 1 else vmem for operand in operands],
        out_specs=jax.tree.map(lambda _: vmem, shapes),
        scratch_shapes=scratch,
        compiler_params=pltpu.CompilerParams(vmem_limit_bytes=VMEM_LIMIT),
        cost_estimate=pl.CostEstimate(flops=flops, bytes_accessed=moved, transcendentals=0),
        name=name,
    )(*operands)


def count_kernel(words_ref, spread_ref, kept_ref):
    rows, width = words_ref.shape
    step = 64

    def chunk(at, totals):
        span = pl.ds(pl.multiple_of(at * step, step), step)
        words = words_ref[span, :]
        kept_ref[span, :] = words
        bits = [
            jnp.bitwise_and(jnp.right_shift(words, 2 * place + bit), 1)
            for bit in range(2)
            for place in range(PLACES)
        ]
        return tuple(
            total + jnp.sum(bit.reshape(step // 8, 8, width), axis=0)
            for total, bit in zip(totals, bits)
        )

    zeros = jnp.zeros((8, width), jnp.int32)
    totals = lax.fori_loop(0, rows // step, chunk, (zeros,) * (2 * PLACES))
    shape = (COUNT_ROWS, width)
    sublane = lax.broadcasted_iota(jnp.int32, shape, 0)
    out = jnp.zeros(shape, jnp.float32)
    for index, total in enumerate(totals):
        count = jnp.sum(total.astype(jnp.float32), axis=0, keepdims=True) - rows / 2
        out = jnp.where(sublane == index, jnp.broadcast_to(count, shape), out)
    out = out.astype(jnp.bfloat16)
    for index in range(spread_ref.shape[0]):
        spread_ref[index] = out


def standardize_kernel(counts_ref, words_ref, weight_ref, variant_ref, matrix_ref):
    rows, width = words_ref.shape
    rows_all = rows * counts_ref.shape[0]
    counts = counts_ref[0].astype(jnp.float32)
    for index in range(1, counts_ref.shape[0]):
        counts = counts + counts_ref[index].astype(jnp.float32)
    counts = counts + rows_all / 2
    ones, twos = counts[:PLACES], counts[PLACES : 2 * PLACES]
    mean = (ones + 2 * twos) / rows_all
    scale = lax.rsqrt((ones + 4 * twos) / rows_all - mean * mean + EPSILON)
    lanes = variant_ref.shape[1]
    step = weight_ref.shape[1]

    def chunk(at, carry):
        span = pl.ds(pl.multiple_of(at * step, step), step)
        weight = jnp.broadcast_to(weight_ref[pl.ds(at, 1), :], (step, step)).T[:, :lanes]
        for place in range(PLACES):
            for first in range(0, width, lanes):
                column = place * width + first
                words = words_ref[span, first : first + lanes]
                dosage = jnp.bitwise_and(jnp.right_shift(words, 2 * place), 3).astype(jnp.float32)
                at_place = (slice(place, place + 1), slice(first, first + lanes))
                variant = variant_ref[column // lanes : column // lanes + 1, :]
                value = (dosage - mean[at_place]) * (scale[at_place] * variant) * weight
                matrix_ref[span, column : column + lanes] = value.astype(jnp.bfloat16)
        return carry

    lax.fori_loop(0, rows // step, chunk, 0)


def sum_spread_kernel(blocks_ref, spread_ref):
    total = blocks_ref[0]
    for index in range(1, blocks_ref.shape[0]):
        total = total + blocks_ref[index]
    total = total.astype(spread_ref.dtype)
    for index in range(spread_ref.shape[0]):
        spread_ref[index] = total


def sum_spread(blocks, count=None, kind=jnp.float32):
    rows, width = blocks.shape[1:]
    shape = jax.ShapeDtypeStruct((count or blocks.shape[0], rows, width), kind)
    return call(sum_spread_kernel, "sum_spread", shape, (blocks,))


def product_kernel(place_ref, gathered_ref, product_ref, spread_ref, gram):
    count = gathered_ref.shape[0]
    own = product_ref.shape[0] // count
    for index in range(count):
        product_ref[index * own : (index + 1) * own] = gathered_ref[index, :own]
    product = product_ref[...]
    gram[...] = lax.dot_general(
        product, product, CONTRACT_ROWS, precision=HIGHEST, preferred_element_type=jnp.float32
    )
    share = gram.shape[0] // NEAR
    rows = gram[pl.ds(pl.multiple_of(place_ref[0] * share, share), share), :]
    for index in range(spread_ref.shape[0]):
        spread_ref[index] = rows


def apply_factor(panel, inverse):
    return lax.dot_general(
        panel, inverse, (((1,), (1,)), ((), ())), precision=HIGHEST, preferred_element_type=jnp.float32
    )


def congruent(gram, factor):
    half = lax.dot_general(
        factor, gram, (((1,), (0,)), ((), ())), precision=HIGHEST, preferred_element_type=jnp.float32
    )
    return apply_factor(half, factor)


def local_gram(panel):
    return lax.dot_general(panel, panel, CONTRACT_ROWS, preferred_element_type=jnp.float32)


def per_device(dosage_words, sample_weight, variant_weight, omega):
    rows_local, width = dosage_words.shape
    rows_all = rows_local * lax.axis_size("row")
    cols_all = PLACES * width * lax.axis_size("col")
    n_row, n_col = lax.axis_size("row"), lax.axis_size("col")
    counts, words = call(
        count_kernel,
        "count",
        (
            jax.ShapeDtypeStruct((n_row, COUNT_ROWS, width), jnp.bfloat16),
            jax.ShapeDtypeStruct((rows_local, width), jnp.int32),
        ),
        (dosage_words,),
    )
    matrix = call(
        standardize_kernel,
        "standardize",
        jax.ShapeDtypeStruct((rows_local, PLACES * width), jnp.bfloat16),
        (
            exchange(counts, "row"),
            words,
            sample_weight.reshape(-1, LANES),
            variant_weight.reshape(-1, LANES),
        ),
    )
    col = lax.axis_index("col")
    own, part = rows_local // n_col, RANK // n_col
    chunk = PLACES * width // n_row

    sketch_part = jnp.dot(matrix, omega, preferred_element_type=jnp.float32)
    arrived = exchange(sketch_part.reshape(n_col, own, RANK), "col")
    sketch = exchange(sum_spread(arrived, kind=jnp.bfloat16), "col").reshape(rows_local, RANK)

    back_part = lax.dot_general(
        matrix, sketch, CONTRACT_ROWS, preferred_element_type=jnp.float32
    ).astype(jnp.bfloat16)
    arrived = exchange(back_part.reshape(n_row, chunk, RANK), "row")
    gram_share = lax.dynamic_slice_in_dim(local_gram(sketch), col * part, part, 0)
    share_terms = jnp.concatenate(
        halves(gram_share, 3) + [jnp.zeros((part, RANK), jnp.bfloat16)], axis=0
    )
    arrived, share_terms = lax.optimization_barrier((arrived, share_terms))
    back_own = jnp.sum(arrived.astype(jnp.float32), axis=0).astype(jnp.bfloat16)
    back_own = jnp.concatenate([back_own, share_terms], axis=0)
    gathered = lax.all_gather(back_own, "row", axis=0, tiled=True)
    gathered = gathered.reshape(n_row, chunk + 4 * part, RANK)
    back = gathered[:, :chunk].reshape(n_row * chunk, RANK)
    gram_share = jnp.sum(
        gathered[:, chunk:].astype(jnp.float32).reshape(4 * n_row, part, RANK), axis=0
    )

    product_part = jnp.dot(matrix, back, preferred_element_type=jnp.float32)
    back_gram = lax.optimization_barrier(local_gram(back))
    arrived = exchange(
        jnp.concatenate(
            [
                product_part.reshape(n_col, own, RANK),
                back_gram.reshape(n_col, part, RANK),
                jnp.broadcast_to(gram_share[None], (n_col, part, RANK)),
            ],
            axis=1,
        ),
        "col",
    )
    sketch_factor = inverse_factor(arrived[:, own + part :].reshape(RANK, RANK))
    gathered = exchange(sum_spread(arrived), "col")
    gathered, sketch_factor = lax.optimization_barrier((gathered, sketch_factor))
    back_gram = gathered[:, own : own + part].reshape(RANK, RANK)

    place = lax.rem(col, NEAR)
    product, spread = call(
        product_kernel,
        "product",
        (
            jax.ShapeDtypeStruct((rows_local, RANK), jnp.float32),
            jax.ShapeDtypeStruct((n_row, RANK // NEAR, RANK), jnp.float32),
        ),
        (place.reshape(1), gathered),
        scratch=[pltpu.VMEM((RANK, RANK), jnp.float32)],
    )
    gathered = exchange(spread, "row")
    back_factor = inverse_factor(back_gram, sketch_factor)
    factor = jnp.dot(back_factor, sketch_factor, precision=HIGHEST)
    right_basis = apply_factor(back.astype(jnp.float32), factor) * math.sqrt(cols_all)
    product = apply_factor(product, factor)
    gathered, product, right_basis = lax.optimization_barrier((gathered, product, right_basis))
    near = [list(range(first, first + NEAR)) for first in range(0, n_col, NEAR)]
    gram = exchange(sum_spread(gathered, count=NEAR), "col", near).reshape(RANK, RANK)
    basis, second = call(
        functools.partial(second_kernel, math.sqrt(rows_all)),
        "second",
        (
            jax.ShapeDtypeStruct((own, RANK), jnp.float32),
            jax.ShapeDtypeStruct((rows_local, RANK), jnp.bfloat16),
        ),
        (col.reshape(1), gram, factor, product),
        scratch=[pltpu.VMEM((RANK, RANK), jnp.float32)] * 2,
    )
    projection_part = lax.dot_general(
        second, matrix, CONTRACT_ROWS, preferred_element_type=jnp.float32
    ).astype(jnp.bfloat16)
    arrived = exchange(projection_part.reshape(n_row, RANK // n_row, -1), "row")
    projection = jnp.sum(arrived.astype(jnp.float32), axis=0).T
    return (basis, right_basis, projection)


def solution(mesh):
    in_specs = (P("row", "col"), P("row"), P("col"), P("col", None))
    out_specs = (P(("row", "col"), None), P("col", None), P("col", "row"))
    return jax.shard_map(
        per_device, mesh=mesh, in_specs=in_specs, out_specs=out_specs, check_vma=False
    )
```

```python
import functools
import math

import jax
import jax.numpy as jnp
from jax import lax
from jax.experimental import pallas as pl
from jax.experimental.pallas import tpu as pltpu
from jax.sharding import PartitionSpec as P

EPSILON = 1e-05
PLACES = 6
RANK = 128
COUNT_ROWS = 16
NEAR = 8
CONTRACT_ROWS = (((0,), (0,)), ((), ()))
HIGHEST = lax.Precision.HIGHEST
VMEM_LIMIT = 32 * 1024 * 1024
BLOCK = 16
SUBLANES, LANES = 8, 128


def exchange(blocks, axis, groups=None):
    return lax.all_to_all(
        blocks, axis, split_axis=0, concat_axis=0, axis_index_groups=groups, tiled=True
    )


def halves(values, count):
    terms = []
    for index in range(count):
        term = lax.reduce_precision(values, exponent_bits=8, mantissa_bits=7)
        values = values - term
        terms.append(term.astype(jnp.bfloat16))
    return terms


def eliminate(inverse_ref, work):
    size = work.shape[0]
    whole, tile = (BLOCK, size), (SUBLANES, size)
    lane = lax.broadcasted_iota(jnp.int32, whole, 1)
    row_at = lax.broadcasted_iota(jnp.int32, whole, 0)
    sublane = lax.broadcasted_iota(jnp.int32, tile, 0)
    all_lanes = lax.broadcasted_iota(jnp.int32, (size, size), 1)

    def spread(rows):
        tiles = []
        for first in range(0, BLOCK, SUBLANES):
            out = rows[first]
            for index in range(1, SUBLANES):
                out = jnp.where(sublane == index, rows[first + index], out)
            tiles.append(out)
        return jnp.concatenate(tiles, axis=0)

    def step(at, carry):
        base = pl.multiple_of(at * BLOCK, BLOCK)
        rows = work[pl.ds(base, BLOCK), :]
        turned = pltpu.roll(rows, lax.rem(size - base, size), 1)
        columns = [jnp.broadcast_to(turned[:, j : j + 1], whole) for j in range(BLOCK)]
        entry = {
            (i, j): jnp.broadcast_to(columns[i][j : j + 1, :], tile)
            for j in range(BLOCK)
            for i in range(j, BLOCK)
        }
        within = jnp.logical_and(lane >= base, lane < base + BLOCK)
        start = jnp.where(within, (lane - base == row_at).astype(jnp.float32), rows)
        done, pivots, reciprocals = [], [], []
        for j in range(BLOCK):
            row = jnp.broadcast_to(start[j : j + 1, :], tile)
            for k in range(j):
                row = row - entry[j, k] * done[k]
            done.append(row)
            pivots.append(entry[j, j])
            reciprocal = 1.0 / entry[j, j]
            reciprocals.append(reciprocal)
            factors = {i: entry[i, j] * reciprocal for i in range(j + 1, BLOCK)}
            for i in range(j + 1, BLOCK):
                for k in range(j + 1, i + 1):
                    entry[i, k] = entry[i, k] - factors[i] * entry[k, j]
            for i in range(j + 1, BLOCK):
                entry[i, j] = factors[i]
        block = spread(done)
        inverse_ref[pl.ds(base, BLOCK), :] = jnp.where(
            lane < base + BLOCK, block, 0.0
        ) * lax.rsqrt(spread(pivots))
        factor = jnp.where(lane >= base + BLOCK, block * spread(reciprocals), 0.0)
        update = lax.dot_general(
            factor, block, CONTRACT_ROWS, precision=HIGHEST, preferred_element_type=jnp.float32
        )
        inside = jnp.logical_and(all_lanes >= base, all_lanes < base + BLOCK)
        work[...] = jnp.where(inside, 0.0, work[...]) - update
        return carry

    lax.fori_loop(0, size // BLOCK, step, 0)


def inverse_factor_kernel(gram_ref, inverse_ref, work):
    work[...] = gram_ref[...]
    eliminate(inverse_ref, work)


def inverse_factor(gram_sum):
    return call(
        inverse_factor_kernel,
        "inverse_factor",
        jax.ShapeDtypeStruct(gram_sum.shape, jnp.float32),
        (gram_sum,),
        scratch=[pltpu.VMEM(gram_sum.shape, jnp.float32)],
        flops=4 * 10**9,
        moved=3 * 10**7,
    )


def back_factor_kernel(
    root,
    gram_ref,
    sketch_factor_ref,
    back_ref,
    product_ref,
    factor_ref,
    right_ref,
    scaled_ref,
    inverse,
    work,
):
    work[...] = congruent(gram_ref[...], sketch_factor_ref[...])
    eliminate(inverse, work)
    factor = lax.dot_general(
        inverse[...],
        sketch_factor_ref[...],
        (((1,), (0,)), ((), ())),
        precision=HIGHEST,
        preferred_element_type=jnp.float32,
    )
    factor_ref[...] = factor
    step = 256

    def right_rows(at, carry):
        span = pl.ds(pl.multiple_of(at * step, step), step)
        right_ref[span, :] = apply_factor(back_ref[span, :].astype(jnp.float32), factor) * root
        return carry

    lax.fori_loop(0, back_ref.shape[0] // step, right_rows, 0)
    scaled_ref[...] = apply_factor(product_ref[...], factor)


def second_kernel(
    root, col_ref, gram_ref, factor_ref, product_ref, own_ref, half_ref, inverse, work
):
    work[...] = congruent(gram_ref[...], factor_ref[...])
    eliminate(inverse, work)
    half_ref[...] = apply_factor(product_ref[...], inverse[...]).astype(jnp.bfloat16)
    own = own_ref.shape[0]
    rows = product_ref[pl.ds(pl.multiple_of(col_ref[0] * own, own), own), :]
    own_ref[...] = apply_factor(rows, inverse[...]) * root


def call(kernel, name, shapes, operands, scratch=(), flops=10**7, moved=4 * 10**6):
    vmem = pl.BlockSpec(memory_space=pltpu.VMEM)
    smem = pl.BlockSpec(memory_space=pltpu.SMEM)
    return pl.pallas_call(
        kernel,
        out_shape=shapes,
        in_specs=[smem if operand.ndim == 1 else vmem for operand in operands],
        out_specs=jax.tree.map(lambda _: vmem, shapes),
        scratch_shapes=scratch,
        compiler_params=pltpu.CompilerParams(vmem_limit_bytes=VMEM_LIMIT),
        cost_estimate=pl.CostEstimate(flops=flops, bytes_accessed=moved, transcendentals=0),
        name=name,
    )(*operands)


def count_kernel(words_ref, weight_ref, variant_ref, spread_ref, kept_ref, *kept):
    kept[0][...] = weight_ref[...]
    kept[1][...] = variant_ref[...]
    rows, width = words_ref.shape
    step = 64

    def chunk(at, totals):
        span = pl.ds(pl.multiple_of(at * step, step), step)
        words = words_ref[span, :]
        kept_ref[span, :] = words
        bits = [
            jnp.bitwise_and(jnp.right_shift(words, 2 * place + bit), 1)
            for bit in range(2)
            for place in range(PLACES)
        ]
        return tuple(
            total + jnp.sum(bit.reshape(step // 8, 8, width), axis=0)
            for total, bit in zip(totals, bits)
        )

    zeros = jnp.zeros((8, width), jnp.int32)
    totals = lax.fori_loop(0, rows // step, chunk, (zeros,) * (2 * PLACES))
    shape = (COUNT_ROWS, width)
    sublane = lax.broadcasted_iota(jnp.int32, shape, 0)
    out = jnp.zeros(shape, jnp.float32)
    for index, total in enumerate(totals):
        count = jnp.sum(total.astype(jnp.float32), axis=0, keepdims=True) - rows / 2
        out = jnp.where(sublane == index, jnp.broadcast_to(count, shape), out)
    out = out.astype(jnp.bfloat16)
    for index in range(spread_ref.shape[0]):
        spread_ref[index] = out


def standardize_kernel(counts_ref, words_ref, weight_ref, variant_ref, matrix_ref):
    rows, width = words_ref.shape
    rows_all = rows * counts_ref.shape[0]
    counts = counts_ref[0].astype(jnp.float32)
    for index in range(1, counts_ref.shape[0]):
        counts = counts + counts_ref[index].astype(jnp.float32)
    counts = counts + rows_all / 2
    ones, twos = counts[:PLACES], counts[PLACES : 2 * PLACES]
    mean = (ones + 2 * twos) / rows_all
    scale = lax.rsqrt((ones + 4 * twos) / rows_all - mean * mean + EPSILON)
    lanes = variant_ref.shape[1]
    step = weight_ref.shape[1]

    def chunk(at, carry):
        span = pl.ds(pl.multiple_of(at * step, step), step)
        weight = jnp.broadcast_to(weight_ref[pl.ds(at, 1), :], (step, step)).T[:, :lanes]
        for place in range(PLACES):
            for first in range(0, width, lanes):
                column = place * width + first
                words = words_ref[span, first : first + lanes]
                dosage = jnp.bitwise_and(jnp.right_shift(words, 2 * place), 3).astype(jnp.float32)
                at_place = (slice(place, place + 1), slice(first, first + lanes))
                variant = variant_ref[column // lanes : column // lanes + 1, :]
                value = (dosage - mean[at_place]) * (scale[at_place] * variant) * weight
                matrix_ref[span, column : column + lanes] = value.astype(jnp.bfloat16)
        return carry

    lax.fori_loop(0, rows // step, chunk, 0)


def sum_spread_kernel(blocks_ref, spread_ref):
    total = blocks_ref[0]
    for index in range(1, blocks_ref.shape[0]):
        total = total + blocks_ref[index]
    total = total.astype(spread_ref.dtype)
    for index in range(spread_ref.shape[0]):
        spread_ref[index] = total


def sum_spread(blocks, count=None, kind=jnp.float32):
    rows, width = blocks.shape[1:]
    shape = jax.ShapeDtypeStruct((count or blocks.shape[0], rows, width), kind)
    return call(sum_spread_kernel, "sum_spread", shape, (blocks,))


def product_kernel(place_ref, gathered_ref, product_ref, spread_ref, gram):
    count = gathered_ref.shape[0]
    own = product_ref.shape[0] // count
    for index in range(count):
        product_ref[index * own : (index + 1) * own] = gathered_ref[index, :own]
    product = product_ref[...]
    gram[...] = lax.dot_general(
        product, product, CONTRACT_ROWS, precision=HIGHEST, preferred_element_type=jnp.float32
    )
    share = gram.shape[0] // NEAR
    rows = gram[pl.ds(pl.multiple_of(place_ref[0] * share, share), share), :]
    for index in range(spread_ref.shape[0]):
        spread_ref[index] = rows


def apply_factor(panel, inverse):
    return lax.dot_general(
        panel, inverse, (((1,), (1,)), ((), ())), precision=HIGHEST, preferred_element_type=jnp.float32
    )


def congruent(gram, factor):
    half = lax.dot_general(
        factor, gram, (((1,), (0,)), ((), ())), precision=HIGHEST, preferred_element_type=jnp.float32
    )
    return apply_factor(half, factor)


def local_gram(panel):
    return lax.dot_general(panel, panel, CONTRACT_ROWS, preferred_element_type=jnp.float32)


def per_device(dosage_words, sample_weight, variant_weight, omega):
    rows_local, width = dosage_words.shape
    rows_all = rows_local * lax.axis_size("row")
    cols_all = PLACES * width * lax.axis_size("col")
    n_row, n_col = lax.axis_size("row"), lax.axis_size("col")
    weights = (sample_weight.reshape(-1, LANES), variant_weight.reshape(-1, LANES))
    counts, *kept = call(
        count_kernel,
        "count",
        (
            jax.ShapeDtypeStruct((n_row, COUNT_ROWS, width), jnp.bfloat16),
            jax.ShapeDtypeStruct(dosage_words.shape, jnp.int32),
            *(jax.ShapeDtypeStruct(weight.shape, jnp.float32) for weight in weights),
        ),
        (dosage_words, *weights),
    )
    matrix = call(
        standardize_kernel,
        "standardize",
        jax.ShapeDtypeStruct((rows_local, PLACES * width), jnp.bfloat16),
        (exchange(counts, "row"), *kept),
    )
    col = lax.axis_index("col")
    own, part = rows_local // n_col, RANK // n_col
    chunk = PLACES * width // n_row

    sketch_part = jnp.dot(matrix, omega, preferred_element_type=jnp.float32)
    arrived = exchange(sketch_part.reshape(n_col, own, RANK), "col")
    sketch = exchange(sum_spread(arrived, kind=jnp.bfloat16), "col").reshape(rows_local, RANK)

    gram_share = lax.dynamic_slice_in_dim(local_gram(sketch), col * part, part, 0)
    share_terms = jnp.concatenate(
        halves(gram_share, 3) + [jnp.zeros((part, RANK), jnp.bfloat16)], axis=0
    )
    back_part = lax.dot_general(
        matrix, sketch, CONTRACT_ROWS, preferred_element_type=jnp.float32
    ).astype(jnp.bfloat16)
    back_part, share_terms = lax.optimization_barrier((back_part, share_terms))
    arrived = exchange(back_part.reshape(n_row, chunk, RANK), "row")
    back_own = jnp.sum(arrived.astype(jnp.float32), axis=0).astype(jnp.bfloat16)
    back_own = jnp.concatenate([back_own, share_terms], axis=0)
    gathered = lax.all_gather(back_own, "row", axis=0, tiled=True)
    gathered = gathered.reshape(n_row, chunk + 4 * part, RANK)
    back = gathered[:, :chunk].reshape(n_row * chunk, RANK)
    gram_share = jnp.sum(
        gathered[:, chunk:].astype(jnp.float32).reshape(4 * n_row, part, RANK), axis=0
    )

    product_part = jnp.dot(matrix, back, preferred_element_type=jnp.float32)
    back_gram = lax.optimization_barrier(local_gram(back))
    arrived = exchange(
        jnp.concatenate(
            [
                product_part.reshape(n_col, own, RANK),
                back_gram.reshape(n_col, part, RANK),
                jnp.broadcast_to(gram_share[None], (n_col, part, RANK)),
            ],
            axis=1,
        ),
        "col",
    )
    sketch_factor = inverse_factor(arrived[:, own + part :].reshape(RANK, RANK))
    gathered = exchange(sum_spread(arrived), "col")
    gathered, sketch_factor = lax.optimization_barrier((gathered, sketch_factor))
    back_gram = gathered[:, own : own + part].reshape(RANK, RANK)

    place = lax.rem(col, NEAR)
    product, spread = call(
        product_kernel,
        "product",
        (
            jax.ShapeDtypeStruct((rows_local, RANK), jnp.float32),
            jax.ShapeDtypeStruct((n_row, RANK // NEAR, RANK), jnp.float32),
        ),
        (place.reshape(1), gathered),
        scratch=[pltpu.VMEM((RANK, RANK), jnp.float32)],
    )
    gathered = exchange(spread, "row")
    factor, right_basis, product = call(
        functools.partial(back_factor_kernel, math.sqrt(cols_all)),
        "back_factor",
        (
            jax.ShapeDtypeStruct((RANK, RANK), jnp.float32),
            jax.ShapeDtypeStruct(back.shape, jnp.float32),
            jax.ShapeDtypeStruct((rows_local, RANK), jnp.float32),
        ),
        (back_gram, sketch_factor, back, product),
        scratch=[pltpu.VMEM((RANK, RANK), jnp.float32)] * 2,
        flops=4 * 10**9,
        moved=3 * 10**7,
    )
    gathered, product = lax.optimization_barrier((gathered, product))
    near = [list(range(first, first + NEAR)) for first in range(0, n_col, NEAR)]
    gram = exchange(sum_spread(gathered, count=NEAR), "col", near).reshape(RANK, RANK)
    basis, second = call(
        functools.partial(second_kernel, math.sqrt(rows_all)),
        "second",
        (
            jax.ShapeDtypeStruct((own, RANK), jnp.float32),
            jax.ShapeDtypeStruct((rows_local, RANK), jnp.bfloat16),
        ),
        (col.reshape(1), gram, factor, product),
        scratch=[pltpu.VMEM((RANK, RANK), jnp.float32)] * 2,
    )
    projection_part = lax.dot_general(
        second, matrix, CONTRACT_ROWS, preferred_element_type=jnp.float32
    ).astype(jnp.bfloat16)
    arrived = exchange(projection_part.reshape(n_row, RANK // n_row, -1), "row")
    projection = jnp.sum(arrived.astype(jnp.float32), axis=0).T
    return (basis, right_basis, projection)


def solution(mesh):
    in_specs = (P("row", "col"), P("row"), P("col"), P("col", None))
    out_specs = (P(("row", "col"), None), P("col", None), P("col", "row"))
    return jax.shard_map(
        per_device, mesh=mesh, in_specs=in_specs, out_specs=out_specs, check_vma=False
    )
```

```python
import functools
import math

import jax
import jax.numpy as jnp
from jax import lax
from jax.experimental import pallas as pl
from jax.experimental.pallas import tpu as pltpu
from jax.sharding import PartitionSpec as P

EPSILON = 1e-05
PLACES = 6
RANK = 128
COUNT_ROWS = 16
NEAR = 8
CONTRACT_ROWS = (((0,), (0,)), ((), ()))
HIGHEST = lax.Precision.HIGHEST
VMEM_LIMIT = 32 * 1024 * 1024
BLOCK = 16
SUBLANES, LANES = 8, 128


def exchange(blocks, axis, groups=None):
    return lax.all_to_all(
        blocks, axis, split_axis=0, concat_axis=0, axis_index_groups=groups, tiled=True
    )


def terms(values, count):
    parts = []
    for index in range(count):
        term = lax.reduce_precision(values, exponent_bits=8, mantissa_bits=7)
        values = values - term
        parts.append(term.astype(jnp.bfloat16))
    return parts


def eliminate(inverse_ref, work):
    size = work.shape[0]
    whole, tile = (BLOCK, size), (SUBLANES, size)
    lane = lax.broadcasted_iota(jnp.int32, whole, 1)
    row_at = lax.broadcasted_iota(jnp.int32, whole, 0)
    sublane = lax.broadcasted_iota(jnp.int32, tile, 0)
    all_lanes = lax.broadcasted_iota(jnp.int32, (size, size), 1)

    def spread(rows):
        tiles = []
        for first in range(0, BLOCK, SUBLANES):
            out = rows[first]
            for index in range(1, SUBLANES):
                out = jnp.where(sublane == index, rows[first + index], out)
            tiles.append(out)
        return jnp.concatenate(tiles, axis=0)

    def step(at, carry):
        base = pl.multiple_of(at * BLOCK, BLOCK)
        rows = work[pl.ds(base, BLOCK), :]
        turned = pltpu.roll(rows, lax.rem(size - base, size), 1)
        columns = [jnp.broadcast_to(turned[:, j : j + 1], whole) for j in range(BLOCK)]
        entry = {
            (i, j): jnp.broadcast_to(columns[i][j : j + 1, :], tile)
            for j in range(BLOCK)
            for i in range(j, BLOCK)
        }
        within = jnp.logical_and(lane >= base, lane < base + BLOCK)
        start = jnp.where(within, (lane - base == row_at).astype(jnp.float32), rows)
        done, pivots, reciprocals = [], [], []
        for j in range(BLOCK):
            row = jnp.broadcast_to(start[j : j + 1, :], tile)
            for k in range(j):
                row = row - entry[j, k] * done[k]
            done.append(row)
            pivots.append(entry[j, j])
            reciprocal = 1.0 / entry[j, j]
            reciprocals.append(reciprocal)
            factors = {i: entry[i, j] * reciprocal for i in range(j + 1, BLOCK)}
            for i in range(j + 1, BLOCK):
                for k in range(j + 1, i + 1):
                    entry[i, k] = entry[i, k] - factors[i] * entry[k, j]
            for i in range(j + 1, BLOCK):
                entry[i, j] = factors[i]
        block = spread(done)
        inverse_ref[pl.ds(base, BLOCK), :] = jnp.where(
            lane < base + BLOCK, block, 0.0
        ) * lax.rsqrt(spread(pivots))
        factor = jnp.where(lane >= base + BLOCK, block * spread(reciprocals), 0.0)
        update = lax.dot_general(
            factor, block, CONTRACT_ROWS, precision=HIGHEST, preferred_element_type=jnp.float32
        )
        inside = jnp.logical_and(all_lanes >= base, all_lanes < base + BLOCK)
        work[...] = jnp.where(inside, 0.0, work[...]) - update
        return carry

    lax.fori_loop(0, size // BLOCK, step, 0)


def inverse_factor_kernel(gram_ref, inverse_ref, work):
    work[...] = gram_ref[...]
    eliminate(inverse_ref, work)


def inverse_factor(gram_sum):
    return call(
        inverse_factor_kernel,
        "inverse_factor",
        jax.ShapeDtypeStruct(gram_sum.shape, jnp.float32),
        (gram_sum,),
        scratch=[pltpu.VMEM(gram_sum.shape, jnp.float32)],
        flops=4 * 10**9,
        moved=3 * 10**7,
    )


def back_factor_kernel(
    root,
    gram_ref,
    sketch_factor_ref,
    back_ref,
    product_ref,
    factor_ref,
    right_ref,
    scaled_ref,
    inverse,
    work,
):
    work[...] = congruent(gram_ref[...], sketch_factor_ref[...])
    eliminate(inverse, work)
    factor = lax.dot_general(
        inverse[...],
        sketch_factor_ref[...],
        (((1,), (0,)), ((), ())),
        precision=HIGHEST,
        preferred_element_type=jnp.float32,
    )
    factor_ref[...] = factor
    step = 256

    def right_rows(at, carry):
        span = pl.ds(pl.multiple_of(at * step, step), step)
        right_ref[span, :] = apply_factor(back_ref[span, :].astype(jnp.float32), factor) * root
        return carry

    lax.fori_loop(0, back_ref.shape[0] // step, right_rows, 0)
    scaled_ref[...] = apply_factor(product_ref[...], factor)


def second_kernel(
    root, col_ref, gram_ref, factor_ref, product_ref, own_ref, half_ref, inverse, work
):
    work[...] = congruent(gram_ref[...], factor_ref[...])
    eliminate(inverse, work)
    half_ref[...] = apply_factor(product_ref[...], inverse[...]).astype(jnp.bfloat16)
    own = own_ref.shape[0]
    rows = product_ref[pl.ds(pl.multiple_of(col_ref[0] * own, own), own), :]
    own_ref[...] = apply_factor(rows, inverse[...]) * root


def call(kernel, name, shapes, operands, scratch=(), flops=10**7, moved=4 * 10**6):
    vmem = pl.BlockSpec(memory_space=pltpu.VMEM)
    smem = pl.BlockSpec(memory_space=pltpu.SMEM)
    return pl.pallas_call(
        kernel,
        out_shape=shapes,
        in_specs=[smem if operand.ndim == 1 else vmem for operand in operands],
        out_specs=jax.tree.map(lambda _: vmem, shapes),
        scratch_shapes=scratch,
        compiler_params=pltpu.CompilerParams(vmem_limit_bytes=VMEM_LIMIT),
        cost_estimate=pl.CostEstimate(flops=flops, bytes_accessed=moved, transcendentals=0),
        name=name,
    )(*operands)


def count_kernel(words_ref, spread_ref, kept_ref):
    rows, width = words_ref.shape
    step = 64

    def chunk(at, totals):
        span = pl.ds(pl.multiple_of(at * step, step), step)
        words = words_ref[span, :]
        kept_ref[span, :] = words
        bits = [
            jnp.bitwise_and(jnp.right_shift(words, 2 * place + bit), 1)
            for bit in range(2)
            for place in range(PLACES)
        ]
        return tuple(
            total + jnp.sum(bit.reshape(step // 8, 8, width), axis=0)
            for total, bit in zip(totals, bits)
        )

    zeros = jnp.zeros((8, width), jnp.int32)
    totals = lax.fori_loop(0, rows // step, chunk, (zeros,) * (2 * PLACES))
    shape = (COUNT_ROWS, width)
    sublane = lax.broadcasted_iota(jnp.int32, shape, 0)
    out = jnp.zeros(shape, jnp.float32)
    for index, total in enumerate(totals):
        count = jnp.sum(total.astype(jnp.float32), axis=0, keepdims=True) - rows / 2
        out = jnp.where(sublane == index, jnp.broadcast_to(count, shape), out)
    out = out.astype(jnp.bfloat16)
    for index in range(spread_ref.shape[0]):
        spread_ref[index] = out


def standardize_kernel(counts_ref, words_ref, weights_ref, matrix_ref):
    rows, width = words_ref.shape
    rows_all = rows * counts_ref.shape[0]
    counts = counts_ref[0].astype(jnp.float32)
    for index in range(1, counts_ref.shape[0]):
        counts = counts + counts_ref[index].astype(jnp.float32)
    counts = counts + rows_all / 2
    ones, twos = counts[:PLACES], counts[PLACES : 2 * PLACES]
    mean = (ones + 2 * twos) / rows_all
    scale = lax.rsqrt((ones + 4 * twos) / rows_all - mean * mean + EPSILON)
    step = lanes = weights_ref.shape[1]

    def chunk(at, carry):
        span = pl.ds(pl.multiple_of(at * step, step), step)
        weight = jnp.broadcast_to(weights_ref[pl.ds(at, 1), :], (step, lanes)).T
        for place in range(PLACES):
            for first in range(0, width, lanes):
                column = place * width + first
                words = words_ref[span, first : first + lanes]
                dosage = jnp.bitwise_and(jnp.right_shift(words, 2 * place), 3).astype(jnp.float32)
                at_place = (slice(place, place + 1), slice(first, first + lanes))
                variant_at = (rows + column) // lanes
                variant = weights_ref[variant_at : variant_at + 1, :]
                value = (dosage - mean[at_place]) * (scale[at_place] * variant) * weight
                matrix_ref[span, column : column + lanes] = value.astype(jnp.bfloat16)
        return carry

    lax.fori_loop(0, rows // step, chunk, 0)


def sum_spread_kernel(blocks_ref, spread_ref):
    total = blocks_ref[0]
    for index in range(1, blocks_ref.shape[0]):
        total = total + blocks_ref[index]
    total = total.astype(spread_ref.dtype)
    for index in range(spread_ref.shape[0]):
        spread_ref[index] = total


def sum_spread(blocks, count=None, kind=jnp.float32):
    rows, width = blocks.shape[1:]
    shape = jax.ShapeDtypeStruct((count or blocks.shape[0], rows, width), kind)
    return call(sum_spread_kernel, "sum_spread", shape, (blocks,))


def product_kernel(place_ref, gathered_ref, product_ref, spread_ref, gram):
    count = gathered_ref.shape[0]
    own = product_ref.shape[0] // count
    for index in range(count):
        product_ref[index * own : (index + 1) * own] = gathered_ref[index, :own]
    product = product_ref[...]
    gram[...] = lax.dot_general(
        product, product, CONTRACT_ROWS, precision=HIGHEST, preferred_element_type=jnp.float32
    )
    share = gram.shape[0] // NEAR
    rows = gram[pl.ds(pl.multiple_of(place_ref[0] * share, share), share), :]
    for index in range(spread_ref.shape[0]):
        spread_ref[index] = rows


def apply_factor(panel, inverse):
    return lax.dot_general(
        panel, inverse, (((1,), (1,)), ((), ())), precision=HIGHEST, preferred_element_type=jnp.float32
    )


def congruent(gram, factor):
    half = lax.dot_general(
        factor, gram, (((1,), (0,)), ((), ())), precision=HIGHEST, preferred_element_type=jnp.float32
    )
    return apply_factor(half, factor)


def local_gram(panel):
    return lax.dot_general(panel, panel, CONTRACT_ROWS, preferred_element_type=jnp.float32)


def per_device(dosage_words, sample_weight, variant_weight, omega):
    rows_local, width = dosage_words.shape
    rows_all = rows_local * lax.axis_size("row")
    cols_all = PLACES * width * lax.axis_size("col")
    n_row, n_col = lax.axis_size("row"), lax.axis_size("col")
    weights = jnp.concatenate(
        [sample_weight.reshape(-1, LANES), variant_weight.reshape(-1, LANES)], axis=0
    )
    dosage_words, weights = lax.optimization_barrier((dosage_words, weights))
    counts, words = call(
        count_kernel,
        "count",
        (
            jax.ShapeDtypeStruct((n_row, COUNT_ROWS, width), jnp.bfloat16),
            jax.ShapeDtypeStruct(dosage_words.shape, jnp.int32),
        ),
        (dosage_words,),
    )
    matrix = call(
        standardize_kernel,
        "standardize",
        jax.ShapeDtypeStruct((rows_local, PLACES * width), jnp.bfloat16),
        (exchange(counts, "row"), words, weights),
    )
    col = lax.axis_index("col")
    own, part = rows_local // n_col, RANK // n_col
    chunk = PLACES * width // n_row

    sketch_part = jnp.dot(matrix, omega, preferred_element_type=jnp.float32)
    arrived = exchange(sketch_part.reshape(n_col, own, RANK), "col")
    sketch = exchange(sum_spread(arrived, kind=jnp.bfloat16), "col").reshape(rows_local, RANK)

    gram_share = lax.dynamic_slice_in_dim(local_gram(sketch), col * part, part, 0)
    share_terms = jnp.concatenate(terms(gram_share, 4), axis=0)
    back_part = lax.dot_general(
        matrix, sketch, CONTRACT_ROWS, preferred_element_type=jnp.float32
    ).astype(jnp.bfloat16)
    back_part, share_terms = lax.optimization_barrier((back_part, share_terms))
    arrived = exchange(back_part.reshape(n_row, chunk, RANK), "row")
    back_own = jnp.sum(arrived.astype(jnp.float32), axis=0).astype(jnp.bfloat16)
    back_own = jnp.concatenate([back_own, share_terms], axis=0)
    gathered = lax.all_gather(back_own, "row", axis=0, tiled=True)
    gathered = gathered.reshape(n_row, chunk + 4 * part, RANK)
    back = gathered[:, :chunk].reshape(n_row * chunk, RANK)
    gram_share = jnp.sum(
        gathered[:, chunk:].astype(jnp.float32).reshape(4 * n_row, part, RANK), axis=0
    )

    product_part = jnp.dot(matrix, back, preferred_element_type=jnp.float32)
    back_gram = lax.optimization_barrier(local_gram(back))
    arrived = exchange(
        jnp.concatenate(
            [
                product_part.reshape(n_col, own, RANK),
                back_gram.reshape(n_col, part, RANK),
                jnp.broadcast_to(gram_share[None], (n_col, part, RANK)),
            ],
            axis=1,
        ),
        "col",
    )
    sketch_factor = inverse_factor(arrived[:, own + part :].reshape(RANK, RANK))
    gathered = exchange(sum_spread(arrived), "col")
    gathered, sketch_factor = lax.optimization_barrier((gathered, sketch_factor))
    back_gram = gathered[:, own : own + part].reshape(RANK, RANK)

    place = lax.rem(col, NEAR)
    product, spread = call(
        product_kernel,
        "product",
        (
            jax.ShapeDtypeStruct((rows_local, RANK), jnp.float32),
            jax.ShapeDtypeStruct((n_row, RANK // NEAR, RANK), jnp.float32),
        ),
        (place.reshape(1), gathered),
        scratch=[pltpu.VMEM((RANK, RANK), jnp.float32)],
    )
    gathered = exchange(spread, "row")
    factor, right_basis, product = call(
        functools.partial(back_factor_kernel, math.sqrt(cols_all)),
        "back_factor",
        (
            jax.ShapeDtypeStruct((RANK, RANK), jnp.float32),
            jax.ShapeDtypeStruct(back.shape, jnp.float32),
            jax.ShapeDtypeStruct((rows_local, RANK), jnp.float32),
        ),
        (back_gram, sketch_factor, back, product),
        scratch=[pltpu.VMEM((RANK, RANK), jnp.float32)] * 2,
        flops=4 * 10**9,
        moved=3 * 10**7,
    )
    gathered, product = lax.optimization_barrier((gathered, product))
    near = [list(range(first, first + NEAR)) for first in range(0, n_col, NEAR)]
    gram = exchange(sum_spread(gathered, count=NEAR), "col", near).reshape(RANK, RANK)
    basis, second = call(
        functools.partial(second_kernel, math.sqrt(rows_all)),
        "second",
        (
            jax.ShapeDtypeStruct((own, RANK), jnp.float32),
            jax.ShapeDtypeStruct((rows_local, RANK), jnp.bfloat16),
        ),
        (col.reshape(1), gram, factor, product),
        scratch=[pltpu.VMEM((RANK, RANK), jnp.float32)] * 2,
    )
    projection_part = lax.dot_general(
        second, matrix, CONTRACT_ROWS, preferred_element_type=jnp.float32
    ).astype(jnp.bfloat16)
    arrived = exchange(projection_part.reshape(n_row, RANK // n_row, -1), "row")
    projection = jnp.sum(arrived.astype(jnp.float32), axis=0).T
    return (basis, right_basis, projection)


def solution(mesh):
    in_specs = (P("row", "col"), P("row"), P("col"), P("col", None))
    out_specs = (P(("row", "col"), None), P("col", None), P("col", "row"))
    return jax.shard_map(
        per_device, mesh=mesh, in_specs=in_specs, out_specs=out_specs, check_vma=False
    )
```

```python
import functools
import math

import jax
import jax.numpy as jnp
from jax import lax
from jax.experimental import pallas as pl
from jax.experimental.pallas import tpu as pltpu
from jax.sharding import PartitionSpec as P

EPSILON = 1e-05
PLACES = 6
RANK = 128
COUNT_ROWS = 16
NEAR = 8
CONTRACT_ROWS = (((0,), (0,)), ((), ()))
HIGHEST = lax.Precision.HIGHEST
VMEM_LIMIT = 32 * 1024 * 1024
BLOCK = 16
SUBLANES, LANES = 8, 128


def exchange(blocks, axis, groups=None):
    return lax.all_to_all(
        blocks, axis, split_axis=0, concat_axis=0, axis_index_groups=groups, tiled=True
    )


def terms(values, count):
    parts = []
    for index in range(count):
        term = lax.reduce_precision(values, exponent_bits=8, mantissa_bits=7)
        values = values - term
        parts.append(term.astype(jnp.bfloat16))
    return parts


def eliminate(inverse_ref, work):
    size = work.shape[0]
    whole, tile = (BLOCK, size), (SUBLANES, size)
    lane = lax.broadcasted_iota(jnp.int32, whole, 1)
    row_at = lax.broadcasted_iota(jnp.int32, whole, 0)
    sublane = lax.broadcasted_iota(jnp.int32, tile, 0)
    all_lanes = lax.broadcasted_iota(jnp.int32, (size, size), 1)

    def spread(rows):
        tiles = []
        for first in range(0, BLOCK, SUBLANES):
            out = rows[first]
            for index in range(1, SUBLANES):
                out = jnp.where(sublane == index, rows[first + index], out)
            tiles.append(out)
        return jnp.concatenate(tiles, axis=0)

    def step(at, carry):
        base = pl.multiple_of(at * BLOCK, BLOCK)
        rows = work[pl.ds(base, BLOCK), :]
        turned = pltpu.roll(rows, lax.rem(size - base, size), 1)
        columns = [jnp.broadcast_to(turned[:, j : j + 1], whole) for j in range(BLOCK)]
        entry = {
            (i, j): jnp.broadcast_to(columns[i][j : j + 1, :], tile)
            for j in range(BLOCK)
            for i in range(j, BLOCK)
        }
        within = jnp.logical_and(lane >= base, lane < base + BLOCK)
        start = jnp.where(within, (lane - base == row_at).astype(jnp.float32), rows)
        done, pivots, reciprocals = [], [], []
        for j in range(BLOCK):
            row = jnp.broadcast_to(start[j : j + 1, :], tile)
            for k in range(j):
                row = row - entry[j, k] * done[k]
            done.append(row)
            pivots.append(entry[j, j])
            reciprocal = 1.0 / entry[j, j]
            reciprocals.append(reciprocal)
            factors = {i: entry[i, j] * reciprocal for i in range(j + 1, BLOCK)}
            for i in range(j + 1, BLOCK):
                for k in range(j + 1, i + 1):
                    entry[i, k] = entry[i, k] - factors[i] * entry[k, j]
            for i in range(j + 1, BLOCK):
                entry[i, j] = factors[i]
        block = spread(done)
        inverse_ref[pl.ds(base, BLOCK), :] = jnp.where(
            lane < base + BLOCK, block, 0.0
        ) * lax.rsqrt(spread(pivots))
        factor = jnp.where(lane >= base + BLOCK, block * spread(reciprocals), 0.0)
        update = lax.dot_general(
            factor, block, CONTRACT_ROWS, precision=HIGHEST, preferred_element_type=jnp.float32
        )
        inside = jnp.logical_and(all_lanes >= base, all_lanes < base + BLOCK)
        work[...] = jnp.where(inside, 0.0, work[...]) - update
        return carry

    lax.fori_loop(0, size // BLOCK, step, 0)


def inverse_factor_kernel(gram_ref, inverse_ref, work):
    work[...] = gram_ref[...]
    eliminate(inverse_ref, work)


def inverse_factor(gram_sum):
    return call(
        inverse_factor_kernel,
        "inverse_factor",
        jax.ShapeDtypeStruct(gram_sum.shape, jnp.float32),
        (gram_sum,),
        scratch=[pltpu.VMEM(gram_sum.shape, jnp.float32)],
        flops=4 * 10**9,
        moved=3 * 10**7,
    )


def back_factor_kernel(
    root,
    gram_ref,
    sketch_factor_ref,
    back_ref,
    product_ref,
    factor_ref,
    right_ref,
    scaled_ref,
    inverse,
    work,
):
    work[...] = congruent(gram_ref[...], sketch_factor_ref[...])
    eliminate(inverse, work)
    factor = lax.dot_general(
        inverse[...],
        sketch_factor_ref[...],
        (((1,), (0,)), ((), ())),
        precision=HIGHEST,
        preferred_element_type=jnp.float32,
    )
    factor_ref[...] = factor
    step = 256

    def right_rows(at, carry):
        span = pl.ds(pl.multiple_of(at * step, step), step)
        right_ref[span, :] = apply_factor(back_ref[span, :].astype(jnp.float32), factor) * root
        return carry

    lax.fori_loop(0, back_ref.shape[0] // step, right_rows, 0)
    scaled_ref[...] = apply_factor(product_ref[...], factor)


def second_kernel(
    root, col_ref, gram_ref, factor_ref, product_ref, own_ref, half_ref, inverse, work
):
    work[...] = congruent(gram_ref[...], factor_ref[...])
    eliminate(inverse, work)
    half_ref[...] = apply_factor(product_ref[...], inverse[...]).astype(jnp.bfloat16)
    own = own_ref.shape[0]
    rows = product_ref[pl.ds(pl.multiple_of(col_ref[0] * own, own), own), :]
    own_ref[...] = apply_factor(rows, inverse[...]) * root


def call(kernel, name, shapes, operands, scratch=(), flops=10**7, moved=4 * 10**6):
    vmem = pl.BlockSpec(memory_space=pltpu.VMEM)
    smem = pl.BlockSpec(memory_space=pltpu.SMEM)
    return pl.pallas_call(
        kernel,
        out_shape=shapes,
        in_specs=[smem if operand.ndim == 1 else vmem for operand in operands],
        out_specs=jax.tree.map(lambda _: vmem, shapes),
        scratch_shapes=scratch,
        compiler_params=pltpu.CompilerParams(vmem_limit_bytes=VMEM_LIMIT),
        cost_estimate=pl.CostEstimate(flops=flops, bytes_accessed=moved, transcendentals=0),
        name=name,
    )(*operands)


def count_kernel(words_ref, spread_ref, kept_ref):
    rows, width = words_ref.shape
    step = 64

    def chunk(at, totals):
        span = pl.ds(pl.multiple_of(at * step, step), step)
        words = words_ref[span, :]
        kept_ref[span, :] = words
        bits = [
            jnp.bitwise_and(jnp.right_shift(words, 2 * place + bit), 1)
            for bit in range(2)
            for place in range(PLACES)
        ]
        return tuple(
            total + jnp.sum(bit.reshape(step // 8, 8, width), axis=0)
            for total, bit in zip(totals, bits)
        )

    zeros = jnp.zeros((8, width), jnp.int32)
    totals = lax.fori_loop(0, rows // step, chunk, (zeros,) * (2 * PLACES))
    shape = (COUNT_ROWS, width)
    sublane = lax.broadcasted_iota(jnp.int32, shape, 0)
    out = jnp.zeros(shape, jnp.float32)
    for index, total in enumerate(totals):
        count = jnp.sum(total.astype(jnp.float32), axis=0, keepdims=True) - rows / 2
        out = jnp.where(sublane == index, jnp.broadcast_to(count, shape), out)
    out = out.astype(jnp.bfloat16)
    for index in range(spread_ref.shape[0]):
        spread_ref[index] = out


def standardize_kernel(counts_ref, words_ref, weights_ref, matrix_ref):
    rows, width = words_ref.shape
    rows_all = rows * counts_ref.shape[0]
    counts = counts_ref[0].astype(jnp.float32)
    for index in range(1, counts_ref.shape[0]):
        counts = counts + counts_ref[index].astype(jnp.float32)
    counts = counts + rows_all / 2
    ones, twos = counts[:PLACES], counts[PLACES : 2 * PLACES]
    mean = (ones + 2 * twos) / rows_all
    scale = lax.rsqrt((ones + 4 * twos) / rows_all - mean * mean + EPSILON)
    step = lanes = weights_ref.shape[1]

    def chunk(at, carry):
        span = pl.ds(pl.multiple_of(at * step, step), step)
        weight = jnp.broadcast_to(weights_ref[pl.ds(at, 1), :], (step, lanes)).T
        for place in range(PLACES):
            for first in range(0, width, lanes):
                column = place * width + first
                words = words_ref[span, first : first + lanes]
                dosage = jnp.bitwise_and(jnp.right_shift(words, 2 * place), 3).astype(jnp.float32)
                at_place = (slice(place, place + 1), slice(first, first + lanes))
                variant_at = (rows + column) // lanes
                variant = weights_ref[variant_at : variant_at + 1, :]
                value = (dosage - mean[at_place]) * (scale[at_place] * variant) * weight
                matrix_ref[span, column : column + lanes] = value.astype(jnp.bfloat16)
        return carry

    lax.fori_loop(0, rows // step, chunk, 0)


def sum_spread_kernel(blocks_ref, spread_ref):
    total = blocks_ref[0].astype(jnp.float32)
    for index in range(1, blocks_ref.shape[0]):
        total = total + blocks_ref[index].astype(jnp.float32)
    total = total.astype(spread_ref.dtype)
    for index in range(spread_ref.shape[0]):
        spread_ref[index] = total


def sum_spread(blocks, count=None, kind=jnp.float32):
    rows, width = blocks.shape[1:]
    shape = jax.ShapeDtypeStruct((count or blocks.shape[0], rows, width), kind)
    return call(sum_spread_kernel, "sum_spread", shape, (blocks,))


def product_kernel(place_ref, gathered_ref, product_ref, spread_ref, gram):
    count = gathered_ref.shape[0]
    own = product_ref.shape[0] // count
    for index in range(count):
        product_ref[index * own : (index + 1) * own] = gathered_ref[index, :own]
    product = product_ref[...]
    gram[...] = lax.dot_general(
        product, product, CONTRACT_ROWS, precision=HIGHEST, preferred_element_type=jnp.float32
    )
    share = gram.shape[0] // NEAR
    rows = gram[pl.ds(pl.multiple_of(place_ref[0] * share, share), share), :]
    for index in range(spread_ref.shape[0]):
        spread_ref[index] = rows


def apply_factor(panel, inverse):
    return lax.dot_general(
        panel, inverse, (((1,), (1,)), ((), ())), precision=HIGHEST, preferred_element_type=jnp.float32
    )


def congruent(gram, factor):
    half = lax.dot_general(
        factor, gram, (((1,), (0,)), ((), ())), precision=HIGHEST, preferred_element_type=jnp.float32
    )
    return apply_factor(half, factor)


def local_gram(panel):
    return lax.dot_general(panel, panel, CONTRACT_ROWS, preferred_element_type=jnp.float32)


def per_device(dosage_words, sample_weight, variant_weight, omega):
    rows_local, width = dosage_words.shape
    rows_all = rows_local * lax.axis_size("row")
    cols_all = PLACES * width * lax.axis_size("col")
    n_row, n_col = lax.axis_size("row"), lax.axis_size("col")
    weights = jnp.concatenate(
        [sample_weight.reshape(-1, LANES), variant_weight.reshape(-1, LANES)], axis=0
    )
    share_at = (lax.axis_index("col") * (RANK // n_col)).astype(jnp.uint32)
    dosage_words, weights, share_at = lax.optimization_barrier((dosage_words, weights, share_at))
    counts, words = call(
        count_kernel,
        "count",
        (
            jax.ShapeDtypeStruct((n_row, COUNT_ROWS, width), jnp.bfloat16),
            jax.ShapeDtypeStruct(dosage_words.shape, jnp.int32),
        ),
        (dosage_words,),
    )
    matrix = call(
        standardize_kernel,
        "standardize",
        jax.ShapeDtypeStruct((rows_local, PLACES * width), jnp.bfloat16),
        (exchange(counts, "row"), words, weights),
    )
    col = lax.axis_index("col")
    own, part = rows_local // n_col, RANK // n_col
    chunk = PLACES * width // n_row

    sketch_part = jnp.dot(matrix, omega, preferred_element_type=jnp.float32).astype(jnp.bfloat16)
    arrived = exchange(sketch_part.reshape(n_col, own, RANK), "col")
    sketch = exchange(sum_spread(arrived, kind=jnp.bfloat16), "col").reshape(rows_local, RANK)

    gram_share = lax.dynamic_slice_in_dim(local_gram(sketch), share_at, part, 0)
    share_terms = jnp.concatenate(terms(gram_share, 4), axis=0)
    back_part = lax.dot_general(
        matrix, sketch, CONTRACT_ROWS, preferred_element_type=jnp.float32
    ).astype(jnp.bfloat16)
    back_part, share_terms = lax.optimization_barrier((back_part, share_terms))
    arrived = exchange(back_part.reshape(n_row, chunk, RANK), "row")
    back_own = jnp.sum(arrived.astype(jnp.float32), axis=0).astype(jnp.bfloat16)
    back_own = jnp.concatenate([back_own, share_terms], axis=0)
    gathered = lax.all_gather(back_own, "row", axis=0, tiled=True)
    gathered = gathered.reshape(n_row, chunk + 4 * part, RANK)
    back = gathered[:, :chunk].reshape(n_row * chunk, RANK)
    gram_share = jnp.sum(
        gathered[:, chunk:].astype(jnp.float32).reshape(4 * n_row, part, RANK), axis=0
    )

    product_part = jnp.dot(matrix, back, preferred_element_type=jnp.float32)
    back_gram = lax.optimization_barrier(local_gram(back))
    arrived = exchange(
        jnp.concatenate(
            [
                product_part.reshape(n_col, own, RANK),
                back_gram.reshape(n_col, part, RANK),
                jnp.broadcast_to(gram_share[None], (n_col, part, RANK)),
            ],
            axis=1,
        ),
        "col",
    )
    sketch_factor = inverse_factor(arrived[:, own + part :].reshape(RANK, RANK))
    gathered = exchange(sum_spread(arrived), "col")
    gathered, sketch_factor = lax.optimization_barrier((gathered, sketch_factor))
    back_gram = gathered[:, own : own + part].reshape(RANK, RANK)

    place = lax.rem(col, NEAR)
    product, spread = call(
        product_kernel,
        "product",
        (
            jax.ShapeDtypeStruct((rows_local, RANK), jnp.float32),
            jax.ShapeDtypeStruct((n_row, RANK // NEAR, RANK), jnp.float32),
        ),
        (place.reshape(1), gathered),
        scratch=[pltpu.VMEM((RANK, RANK), jnp.float32)],
    )
    gathered = exchange(spread, "row")
    factor, right_basis, product = call(
        functools.partial(back_factor_kernel, math.sqrt(cols_all)),
        "back_factor",
        (
            jax.ShapeDtypeStruct((RANK, RANK), jnp.float32),
            jax.ShapeDtypeStruct(back.shape, jnp.float32),
            jax.ShapeDtypeStruct((rows_local, RANK), jnp.float32),
        ),
        (back_gram, sketch_factor, back, product),
        scratch=[pltpu.VMEM((RANK, RANK), jnp.float32)] * 2,
        flops=4 * 10**9,
        moved=3 * 10**7,
    )
    gathered, product = lax.optimization_barrier((gathered, product))
    near = [list(range(first, first + NEAR)) for first in range(0, n_col, NEAR)]
    gram = exchange(sum_spread(gathered, count=NEAR), "col", near).reshape(RANK, RANK)
    basis, second = call(
        functools.partial(second_kernel, math.sqrt(rows_all)),
        "second",
        (
            jax.ShapeDtypeStruct((own, RANK), jnp.float32),
            jax.ShapeDtypeStruct((rows_local, RANK), jnp.bfloat16),
        ),
        (col.reshape(1), gram, factor, product),
        scratch=[pltpu.VMEM((RANK, RANK), jnp.float32)] * 2,
    )
    projection_part = lax.dot_general(
        second, matrix, CONTRACT_ROWS, preferred_element_type=jnp.float32
    ).astype(jnp.bfloat16)
    arrived = exchange(projection_part.reshape(n_row, RANK // n_row, -1), "row")
    projection = jnp.sum(arrived.astype(jnp.float32), axis=0).T
    return (basis, right_basis, projection)


def solution(mesh):
    in_specs = (P("row", "col"), P("row"), P("col"), P("col", None))
    out_specs = (P(("row", "col"), None), P("col", None), P("col", "row"))
    return jax.shard_map(
        per_device, mesh=mesh, in_specs=in_specs, out_specs=out_specs, check_vma=False
    )
```

```python
import functools
import math

import jax
import jax.numpy as jnp
from jax import lax
from jax.experimental import pallas as pl
from jax.experimental.pallas import tpu as pltpu
from jax.sharding import PartitionSpec as P

EPSILON = 1e-05
PLACES = 6
RANK = 128
COUNT_ROWS = 16
NEAR = 8
CONTRACT_ROWS = (((0,), (0,)), ((), ()))
HIGHEST = lax.Precision.HIGHEST
VMEM_LIMIT = 32 * 1024 * 1024
BLOCK = 32
SUBLANES, LANES = 8, 128


def exchange(blocks, axis, groups=None):
    return lax.all_to_all(
        blocks, axis, split_axis=0, concat_axis=0, axis_index_groups=groups, tiled=True
    )


def terms(values, count):
    parts = []
    for index in range(count):
        term = lax.reduce_precision(values, exponent_bits=8, mantissa_bits=7)
        values = values - term
        parts.append(term.astype(jnp.bfloat16))
    return parts


def eliminate(inverse_ref, work):
    size = work.shape[0]
    whole, tile = (BLOCK, size), (SUBLANES, size)
    lane = lax.broadcasted_iota(jnp.int32, whole, 1)
    row_at = lax.broadcasted_iota(jnp.int32, whole, 0)
    sublane = lax.broadcasted_iota(jnp.int32, tile, 0)
    all_lanes = lax.broadcasted_iota(jnp.int32, (size, size), 1)

    def spread(rows):
        tiles = []
        for first in range(0, BLOCK, SUBLANES):
            out = rows[first]
            for index in range(1, SUBLANES):
                out = jnp.where(sublane == index, rows[first + index], out)
            tiles.append(out)
        return jnp.concatenate(tiles, axis=0)

    def step(at, carry):
        base = pl.multiple_of(at * BLOCK, BLOCK)
        rows = work[pl.ds(base, BLOCK), :]
        turned = pltpu.roll(rows, lax.rem(size - base, size), 1)
        columns = [jnp.broadcast_to(turned[:, j : j + 1], whole) for j in range(BLOCK)]
        entry = {
            (i, j): jnp.broadcast_to(columns[i][j : j + 1, :], tile)
            for j in range(BLOCK)
            for i in range(j, BLOCK)
        }
        within = jnp.logical_and(lane >= base, lane < base + BLOCK)
        start = jnp.where(within, (lane - base == row_at).astype(jnp.float32), rows)
        done, pivots, reciprocals = [], [], []
        for j in range(BLOCK):
            row = jnp.broadcast_to(start[j : j + 1, :], tile)
            for k in range(j):
                row = row - entry[j, k] * done[k]
            done.append(row)
            pivots.append(entry[j, j])
            reciprocal = 1.0 / entry[j, j]
            reciprocals.append(reciprocal)
            factors = {i: entry[i, j] * reciprocal for i in range(j + 1, BLOCK)}
            for i in range(j + 1, BLOCK):
                for k in range(j + 1, i + 1):
                    entry[i, k] = entry[i, k] - factors[i] * entry[k, j]
            for i in range(j + 1, BLOCK):
                entry[i, j] = factors[i]
        block = spread(done)
        inverse_ref[pl.ds(base, BLOCK), :] = jnp.where(
            lane < base + BLOCK, block, 0.0
        ) * lax.rsqrt(spread(pivots))
        factor = jnp.where(lane >= base + BLOCK, block * spread(reciprocals), 0.0)
        update = lax.dot_general(
            factor, block, CONTRACT_ROWS, precision=HIGHEST, preferred_element_type=jnp.float32
        )
        inside = jnp.logical_and(all_lanes >= base, all_lanes < base + BLOCK)
        work[...] = jnp.where(inside, 0.0, work[...]) - update
        return carry

    lax.fori_loop(0, size // BLOCK, step, 0)


def inverse_factor_kernel(gram_ref, inverse_ref, work):
    work[...] = gram_ref[...]
    eliminate(inverse_ref, work)


def inverse_factor(gram_sum):
    return call(
        inverse_factor_kernel,
        "inverse_factor",
        jax.ShapeDtypeStruct(gram_sum.shape, jnp.float32),
        (gram_sum,),
        scratch=[pltpu.VMEM(gram_sum.shape, jnp.float32)],
        flops=4 * 10**9,
        moved=3 * 10**7,
    )


def back_factor_kernel(
    root,
    gram_ref,
    sketch_factor_ref,
    back_ref,
    product_ref,
    factor_ref,
    right_ref,
    scaled_ref,
    inverse,
    work,
):
    work[...] = congruent(gram_ref[...], sketch_factor_ref[...])
    eliminate(inverse, work)
    factor = lax.dot_general(
        inverse[...],
        sketch_factor_ref[...],
        (((1,), (0,)), ((), ())),
        precision=HIGHEST,
        preferred_element_type=jnp.float32,
    )
    factor_ref[...] = factor
    step = 256

    def right_rows(at, carry):
        span = pl.ds(pl.multiple_of(at * step, step), step)
        right_ref[span, :] = apply_factor(back_ref[span, :].astype(jnp.float32), factor) * root
        return carry

    lax.fori_loop(0, back_ref.shape[0] // step, right_rows, 0)
    scaled_ref[...] = apply_factor(product_ref[...], factor)


def second_kernel(
    root, col_ref, gram_ref, factor_ref, product_ref, own_ref, half_ref, inverse, work
):
    work[...] = congruent(gram_ref[...], factor_ref[...])
    eliminate(inverse, work)
    half_ref[...] = apply_factor(product_ref[...], inverse[...]).astype(jnp.bfloat16)
    own = own_ref.shape[0]
    rows = product_ref[pl.ds(pl.multiple_of(col_ref[0] * own, own), own), :]
    own_ref[...] = apply_factor(rows, inverse[...]) * root


def call(kernel, name, shapes, operands, scratch=(), flops=10**7, moved=4 * 10**6):
    vmem = pl.BlockSpec(memory_space=pltpu.VMEM)
    smem = pl.BlockSpec(memory_space=pltpu.SMEM)
    return pl.pallas_call(
        kernel,
        out_shape=shapes,
        in_specs=[smem if operand.ndim == 1 else vmem for operand in operands],
        out_specs=jax.tree.map(lambda _: vmem, shapes),
        scratch_shapes=scratch,
        compiler_params=pltpu.CompilerParams(vmem_limit_bytes=VMEM_LIMIT),
        cost_estimate=pl.CostEstimate(flops=flops, bytes_accessed=moved, transcendentals=0),
        name=name,
    )(*operands)


def count_kernel(words_ref, spread_ref, kept_ref):
    rows, width = words_ref.shape
    step = 64

    def chunk(at, totals):
        span = pl.ds(pl.multiple_of(at * step, step), step)
        words = words_ref[span, :]
        kept_ref[span, :] = words
        bits = [
            jnp.bitwise_and(jnp.right_shift(words, 2 * place + bit), 1)
            for bit in range(2)
            for place in range(PLACES)
        ]
        return tuple(
            total + jnp.sum(bit.reshape(step // 8, 8, width), axis=0)
            for total, bit in zip(totals, bits)
        )

    zeros = jnp.zeros((8, width), jnp.int32)
    totals = lax.fori_loop(0, rows // step, chunk, (zeros,) * (2 * PLACES))
    shape = (COUNT_ROWS, width)
    sublane = lax.broadcasted_iota(jnp.int32, shape, 0)
    out = jnp.zeros(shape, jnp.float32)
    for index, total in enumerate(totals):
        count = jnp.sum(total.astype(jnp.float32), axis=0, keepdims=True) - rows / 2
        out = jnp.where(sublane == index, jnp.broadcast_to(count, shape), out)
    out = out.astype(jnp.bfloat16)
    for index in range(spread_ref.shape[0]):
        spread_ref[index] = out


def standardize_kernel(counts_ref, words_ref, weights_ref, matrix_ref):
    rows, width = words_ref.shape
    rows_all = rows * counts_ref.shape[0]
    counts = counts_ref[0].astype(jnp.float32)
    for index in range(1, counts_ref.shape[0]):
        counts = counts + counts_ref[index].astype(jnp.float32)
    counts = counts + rows_all / 2
    ones, twos = counts[:PLACES], counts[PLACES : 2 * PLACES]
    mean = (ones + 2 * twos) / rows_all
    scale = lax.rsqrt((ones + 4 * twos) / rows_all - mean * mean + EPSILON)
    step = lanes = weights_ref.shape[1]

    def chunk(at, carry):
        span = pl.ds(pl.multiple_of(at * step, step), step)
        weight = jnp.broadcast_to(weights_ref[pl.ds(at, 1), :], (step, lanes)).T
        for place in range(PLACES):
            for first in range(0, width, lanes):
                column = place * width + first
                words = words_ref[span, first : first + lanes]
                dosage = jnp.bitwise_and(jnp.right_shift(words, 2 * place), 3).astype(jnp.float32)
                at_place = (slice(place, place + 1), slice(first, first + lanes))
                variant_at = (rows + column) // lanes
                variant = weights_ref[variant_at : variant_at + 1, :]
                value = (dosage - mean[at_place]) * (scale[at_place] * variant) * weight
                matrix_ref[span, column : column + lanes] = value.astype(jnp.bfloat16)
        return carry

    lax.fori_loop(0, rows // step, chunk, 0)


def sum_spread_kernel(blocks_ref, spread_ref):
    total = blocks_ref[0].astype(jnp.float32)
    for index in range(1, blocks_ref.shape[0]):
        total = total + blocks_ref[index].astype(jnp.float32)
    total = total.astype(spread_ref.dtype)
    for index in range(spread_ref.shape[0]):
        spread_ref[index] = total


def sum_spread(blocks, count=None, kind=jnp.float32):
    rows, width = blocks.shape[1:]
    shape = jax.ShapeDtypeStruct((count or blocks.shape[0], rows, width), kind)
    return call(sum_spread_kernel, "sum_spread", shape, (blocks,))


def product_kernel(place_ref, gathered_ref, product_ref, spread_ref, gram):
    count = gathered_ref.shape[0]
    own = product_ref.shape[0] // count
    for index in range(count):
        product_ref[index * own : (index + 1) * own] = gathered_ref[index, :own]
    product = product_ref[...]
    gram[...] = lax.dot_general(
        product, product, CONTRACT_ROWS, precision=HIGHEST, preferred_element_type=jnp.float32
    )
    share = gram.shape[0] // NEAR
    rows = gram[pl.ds(pl.multiple_of(place_ref[0] * share, share), share), :]
    for index in range(spread_ref.shape[0]):
        spread_ref[index] = rows


def apply_factor(panel, inverse):
    return lax.dot_general(
        panel, inverse, (((1,), (1,)), ((), ())), precision=HIGHEST, preferred_element_type=jnp.float32
    )


def congruent(gram, factor):
    half = lax.dot_general(
        factor, gram, (((1,), (0,)), ((), ())), precision=HIGHEST, preferred_element_type=jnp.float32
    )
    return apply_factor(half, factor)


def local_gram(panel):
    return lax.dot_general(panel, panel, CONTRACT_ROWS, preferred_element_type=jnp.float32)


def per_device(dosage_words, sample_weight, variant_weight, omega):
    rows_local, width = dosage_words.shape
    rows_all = rows_local * lax.axis_size("row")
    cols_all = PLACES * width * lax.axis_size("col")
    n_row, n_col = lax.axis_size("row"), lax.axis_size("col")
    weights = jnp.concatenate(
        [sample_weight.reshape(-1, LANES), variant_weight.reshape(-1, LANES)], axis=0
    )
    share_at = (lax.axis_index("col") * (RANK // n_col)).astype(jnp.uint32)
    dosage_words, weights, share_at = lax.optimization_barrier((dosage_words, weights, share_at))
    counts, words = call(
        count_kernel,
        "count",
        (
            jax.ShapeDtypeStruct((n_row, COUNT_ROWS, width), jnp.bfloat16),
            jax.ShapeDtypeStruct(dosage_words.shape, jnp.int32),
        ),
        (dosage_words,),
    )
    matrix = call(
        standardize_kernel,
        "standardize",
        jax.ShapeDtypeStruct((rows_local, PLACES * width), jnp.bfloat16),
        (exchange(counts, "row"), words, weights),
    )
    col = lax.axis_index("col")
    own, part = rows_local // n_col, RANK // n_col
    chunk = PLACES * width // n_row

    sketch_part = jnp.dot(matrix, omega, preferred_element_type=jnp.float32).astype(jnp.bfloat16)
    arrived = exchange(sketch_part.reshape(n_col, own, RANK), "col")
    sketch = exchange(sum_spread(arrived, kind=jnp.bfloat16), "col").reshape(rows_local, RANK)

    gram_share = lax.dynamic_slice_in_dim(local_gram(sketch), share_at, part, 0)
    share_terms = jnp.concatenate(terms(gram_share, 4), axis=0)
    back_part = lax.dot_general(
        matrix, sketch, CONTRACT_ROWS, preferred_element_type=jnp.float32
    ).astype(jnp.bfloat16)
    back_part, share_terms = lax.optimization_barrier((back_part, share_terms))
    arrived = exchange(back_part.reshape(n_row, chunk, RANK), "row")
    back_own = jnp.sum(arrived.astype(jnp.float32), axis=0).astype(jnp.bfloat16)
    back_own = jnp.concatenate([back_own, share_terms], axis=0)
    gathered = lax.all_gather(back_own, "row", axis=0, tiled=True)
    gathered = gathered.reshape(n_row, chunk + 4 * part, RANK)
    back = gathered[:, :chunk].reshape(n_row * chunk, RANK)
    gram_share = jnp.sum(
        gathered[:, chunk:].astype(jnp.float32).reshape(4 * n_row, part, RANK), axis=0
    )

    product_part = jnp.dot(matrix, back, preferred_element_type=jnp.float32)
    back_gram = lax.optimization_barrier(local_gram(back))
    arrived = exchange(
        jnp.concatenate(
            [
                product_part.reshape(n_col, own, RANK),
                back_gram.reshape(n_col, part, RANK),
                jnp.broadcast_to(gram_share[None], (n_col, part, RANK)),
            ],
            axis=1,
        ),
        "col",
    )
    sketch_factor = inverse_factor(arrived[:, own + part :].reshape(RANK, RANK))
    gathered = exchange(sum_spread(arrived), "col")
    gathered, sketch_factor = lax.optimization_barrier((gathered, sketch_factor))
    back_gram = gathered[:, own : own + part].reshape(RANK, RANK)

    place = lax.rem(col, NEAR)
    product, spread = call(
        product_kernel,
        "product",
        (
            jax.ShapeDtypeStruct((rows_local, RANK), jnp.float32),
            jax.ShapeDtypeStruct((n_row, RANK // NEAR, RANK), jnp.float32),
        ),
        (place.reshape(1), gathered),
        scratch=[pltpu.VMEM((RANK, RANK), jnp.float32)],
    )
    gathered = exchange(spread, "row")
    factor, right_basis, product = call(
        functools.partial(back_factor_kernel, math.sqrt(cols_all)),
        "back_factor",
        (
            jax.ShapeDtypeStruct((RANK, RANK), jnp.float32),
            jax.ShapeDtypeStruct(back.shape, jnp.float32),
            jax.ShapeDtypeStruct((rows_local, RANK), jnp.float32),
        ),
        (back_gram, sketch_factor, back, product),
        scratch=[pltpu.VMEM((RANK, RANK), jnp.float32)] * 2,
        flops=4 * 10**9,
        moved=3 * 10**7,
    )
    gathered, product = lax.optimization_barrier((gathered, product))
    near = [list(range(first, first + NEAR)) for first in range(0, n_col, NEAR)]
    gram = exchange(sum_spread(gathered, count=NEAR), "col", near).reshape(RANK, RANK)
    basis, second = call(
        functools.partial(second_kernel, math.sqrt(rows_all)),
        "second",
        (
            jax.ShapeDtypeStruct((own, RANK), jnp.float32),
            jax.ShapeDtypeStruct((rows_local, RANK), jnp.bfloat16),
        ),
        (col.reshape(1), gram, factor, product),
        scratch=[pltpu.VMEM((RANK, RANK), jnp.float32)] * 2,
    )
    projection_part = lax.dot_general(
        second, matrix, CONTRACT_ROWS, preferred_element_type=jnp.float32
    ).astype(jnp.bfloat16)
    arrived = exchange(projection_part.reshape(n_row, RANK // n_row, -1), "row")
    projection = jnp.sum(arrived.astype(jnp.float32), axis=0).T
    return (basis, right_basis, projection)


def solution(mesh):
    in_specs = (P("row", "col"), P("row"), P("col"), P("col", None))
    out_specs = (P(("row", "col"), None), P("col", None), P("col", "row"))
    return jax.shard_map(
        per_device, mesh=mesh, in_specs=in_specs, out_specs=out_specs, check_vma=False
    )
```
